512 devices in a mesh: inst: 64 (over y_lo, x, z), tp: 8 (over y_hi, core).
Axes of the slice: x: 4, y: 8 (y_hi: 4, y_lo: 2; y = y_hi * 2 + y_lo), z: 8, core: 2. Of those that a mesh axis runs over, the one named last changes fastest.
Arguments:
- queries: bfloat16 [512, 8192], P('inst', 'tp'), as said below
- new_kv: bfloat16 [512, 2048], P('inst', 'tp'), may hold values from -6 to 6
- cache: bfloat16 [512, 1024, 2048], P('inst', None, 'tp'), as said below
- lengths: int32 [512], P('inst'), may hold values from 128 to 1024, as said below
- migrate_slot: int32 [64], P('inst'), may hold values from 0 to 7
- pool: bfloat16 [512, 128, 2048], P('inst', None, 'tp'), may hold values from -6 to 6
- prefix_blocks: int32 [512, 16], P('inst'), may hold values from -1 to 511, as said below
Outputs:
- attended: bfloat16 [512, 8192], P(('inst', 'tp'))
The draws below stay inside these ranges and needn't reach their ends.
Inputs may be any that keep to these rules, and one draw needn't show every extreme that they name: `queries`: query entries lie in -6 to 6. `cache`: cache entries lie in -6 to 6. `lengths`: each instance has a slot of length 1024. `prefix_blocks`: in each row the valid ids come first, then -1; more than half of a row's 16 entries are valid. Over the 8 rows of one instance, every owner (id // 8) is named at least once and at most 2 times, and some owner exactly 2 times.
All inputs are finite; a program needn't handle non-finite values.
Results may differ from the reference program's by a relative error of at most 0.013.
Values may be sent and summed in bfloat16 or wider, within the bound.
No kernel may reach another device: no remote copies, remote signals or barrier semaphores. Data moves between devices by JAX's collectives and lax.ppermute only.
A program may use at most 64 MiB of HBM per device.

```python
import jax
import jax.numpy as jnp
from jax import lax

QH = 64
KVH = 8
HD = 128
R = 8
LMAX = 1024
BLK = 128
POOL = 8
NPB = 16
REQS = 512
N_INST = 64


def draw_queries(key, part):
    key = jax.random.fold_in(key, 11)
    base_key = jax.random.fold_in(key, 0)
    shape = (REQS, KVH, QH // KVH, HD)
    entries = jnp.clip(jax.random.normal(base_key, shape, jnp.float32), -6.0, 6.0)
    return entries.reshape(REQS, QH * HD).astype(jnp.bfloat16)


def draw_cache(key, part):
    key = jax.random.fold_in(key, 13)
    shape = (REQS, LMAX, KVH, 2, HD)
    entries = jnp.clip(jax.random.normal(key, shape, jnp.float32), -6.0, 6.0)
    return entries.reshape(REQS, LMAX, KVH * 2 * HD).astype(jnp.bfloat16)


def draw_lengths(key, part):
    key = jax.random.fold_in(key, 17)
    length_key, slot_key = jax.random.split(key)
    drawn = jax.random.randint(length_key, (N_INST, R), LMAX // 8, LMAX + 1)
    longest = jax.random.randint(slot_key, (N_INST, 1), 0, R)
    filled = jnp.where(jnp.arange(R)[None, :] == longest, LMAX, drawn)
    return filled.reshape(REQS).astype(jnp.int32)


def draw_prefix_blocks(key, part):
    key = jax.random.fold_in(key, 19)
    count_key, owner_key, local_key = jax.random.split(key, 3)
    entry_count = R * NPB
    counts = jax.random.randint(count_key, (N_INST, R), NPB // 2 + 1, NPB + 1)
    valid_mask = jnp.arange(NPB)[None, None, :] < counts[:, :, None]
    flat_valid = valid_mask.reshape(N_INST, entry_count).astype(jnp.int32)
    valid_rank = jnp.cumsum(flat_valid, axis=1) - 1
    owner_perms = jax.vmap(lambda sub_key: jax.random.permutation(sub_key, N_INST))(jax.random.split(owner_key, N_INST))
    owner_id = jnp.take_along_axis(owner_perms, jnp.mod(valid_rank, N_INST), axis=1)
    local_id = jax.random.randint(local_key, (N_INST, entry_count), 0, POOL)
    block_ids = jnp.where(flat_valid > 0, owner_id * POOL + local_id, -1)
    return block_ids.reshape(REQS, NPB).astype(jnp.int32)


def place_ends(array, key, low, largest):
    longest = array.shape.index(max(array.shape))
    spots = []
    for shift in (0, 1):
        where = [jax.random.randint(jax.random.fold_in(key, axis), (), 0, length) for axis, length in enumerate(array.shape)]
        where[longest] = (where[longest] + shift) % array.shape[longest]
        spots.append(tuple(where))
    return array.at[spots[0]].set(low).at[spots[1]].set(largest)


def block_levels(rng, shape, cuts, low, high):
    factor_of, own = 1.0, jax.random.fold_in(rng, 6)
    for axis_at, shards_of in cuts:
        steps = jnp.exp(jax.random.uniform(jax.random.fold_in(own, axis_at), (shards_of,), jnp.float32, low / len(cuts), high / len(cuts)))
        factor_of = factor_of * jnp.repeat(steps, shape[axis_at] // shards_of).reshape([-1 if axis == axis_at else 1 for axis in range(len(shape))])
    return factor_of


def noise(key, extent, width, reach, cuts=(), kind=jnp.bfloat16):
    entries = width * jax.random.normal(key, extent, jnp.float32)
    if cuts:
        entries = entries * block_levels(key, extent, cuts, -0.22, 0.18)
    return jnp.clip(entries, -reach, reach).astype(kind)


def setup_inputs(seed: int = 0) -> dict:
    keys = jax.random.split(jax.random.key(seed), 8)
    return {
        "queries": draw_queries(jax.random.fold_in(keys[7], 71), 0),
        "new_kv": noise(keys[1], (REQS, KVH * 2 * HD), 1.0, 6.0, ((0, 64), (1, 8))),
        "cache": draw_cache(jax.random.fold_in(keys[7], 71), 0),
        "lengths": draw_lengths(jax.random.fold_in(keys[7], 71), 0),
        "migrate_slot": place_ends(jax.random.randint(keys[4], (N_INST,), 0, R), jax.random.fold_in(keys[4], 1), 0, R - 1).astype(jnp.int32),
        "pool": noise(keys[5], (N_INST * POOL, BLK, KVH * 2 * HD), 1.0, 6.0, ((0, 64), (2, 8))),
        "prefix_blocks": draw_prefix_blocks(jax.random.fold_in(keys[7], 71), 0),
    }


MASK_VALUE = -1.0e30


def block_partials(query_row, blocks, valid_mask):
    head_width = query_row.shape[-1]
    key_part = blocks[..., :head_width].astype(jnp.float32)
    value_part = blocks[..., head_width:].astype(jnp.float32)
    scores = jnp.einsum("hgd,bthd->bhgt", query_row, key_part) * (head_width ** -0.5)
    keep_mask = valid_mask[:, None, None, :]
    peak_score = jnp.max(jnp.where(keep_mask, scores, MASK_VALUE), axis=-1)
    weights = jnp.where(keep_mask, jnp.exp(scores - peak_score[..., None]), 0.0)
    weight_sum = jnp.sum(weights, axis=-1)
    rounded = lax.optimization_barrier(weights.astype(jnp.bfloat16)).astype(jnp.float32)
    blended = jnp.einsum("bhgt,bthd->bhgd", rounded, value_part)
    return peak_score, weight_sum, blended


def reference(queries, new_kv, cache, lengths, migrate_slot, pool, prefix_blocks):
    group_count = QH // KVH
    span_count = LMAX // BLK
    request_ids = jnp.arange(REQS, dtype=jnp.int32)
    instance = request_ids // R
    partner = jnp.bitwise_xor(instance, N_INST // 2).astype(jnp.int32)
    moving = (request_ids % R) == migrate_slot[instance]
    source = jnp.where(moving, partner * R + migrate_slot[partner], request_ids).astype(jnp.int32)
    stamps = jnp.arange(LMAX, dtype=jnp.int32).reshape(span_count, BLK)
    pool_blocks = pool.reshape(N_INST * POOL, BLK, KVH, 2 * HD)

    def per_request(request):
        query_row = queries[request].reshape(KVH, group_count, HD).astype(jnp.float32)
        anchor = source[request]
        resident = cache[anchor].reshape(span_count, BLK, KVH, 2 * HD)
        resident_part = block_partials(query_row, resident, stamps < lengths[anchor])
        listed = prefix_blocks[request]
        fetched = pool_blocks[jnp.maximum(listed, 0).astype(jnp.int32)]
        listed_mask = jnp.broadcast_to((listed >= 0)[:, None], (listed.shape[0], BLK))
        prefix_part = block_partials(query_row, fetched, listed_mask)
        fresh_mask = jnp.zeros((1, 1), jnp.int32) == 0
        fresh_part = block_partials(query_row, new_kv[request].reshape(1, 1, KVH, 2 * HD), fresh_mask)
        peak_all = jnp.concatenate([resident_part[0], prefix_part[0], fresh_part[0]], axis=0)
        sum_all = jnp.concatenate([resident_part[1], prefix_part[1], fresh_part[1]], axis=0)
        blend_all = jnp.concatenate([resident_part[2], prefix_part[2], fresh_part[2]], axis=0)
        top_score = jnp.max(peak_all, axis=0)
        block_scale = jnp.exp(peak_all - top_score[None])
        numerator = jnp.sum(block_scale[..., None] * blend_all, axis=0)
        denominator = jnp.sum(block_scale * sum_all, axis=0)
        return (numerator / denominator[..., None]).astype(jnp.bfloat16).reshape(-1)

    return lax.map(per_request, request_ids)
```

```python
import jax
import jax.numpy as jnp
from jax import lax
from jax.experimental import pallas as pl
from jax.experimental.pallas import tpu as pltpu
from jax.sharding import PartitionSpec as P

QH = 64
KVH = 8
HD = 128
BLK = 128
GRP = QH // KVH
CAP = 2
NONE = 8191
FIRST = 20
FIRST_TP = 4
TAIL = 16
HEADS = 2
TOGETHER = 4
ROWS = 18
SCALE = HD**-0.5
LOW = -1e30
MIB = 1024 * 1024

NT = (((1,), (1,)), ((), ()))
NN = (((1,), (0,)), ((), ()))


def dot(a, b, dims):
    return lax.dot_general(a, b, dims, preferred_element_type=jnp.float32)


def in_hbm(x):
    return pltpu.with_memory_space_constraint(x, pltpu.HBM)


def lanes(shape):
    return lax.broadcasted_iota(jnp.int32, shape, len(shape) - 1)


def slot_codes(ids, insts):
    rows, width = ids.shape
    slots = CAP * insts
    lane = (lanes((rows, slots)) & (insts - 1)) ^ FIRST
    row = lax.broadcasted_iota(jnp.int32, (rows, slots), 0)
    first = jnp.full((rows, slots), NONE, jnp.int32)
    last = jnp.full((rows, slots), -1, jnp.int32)
    for e in range(width):
        entry = jnp.broadcast_to(ids[:, e : e + 1], (rows, slots))
        named = (entry >= 0) & ((entry >> 3) == lane)
        code = (row * width + e) * 8 + (entry & 7)
        first = jnp.where(named, jnp.minimum(first, code), first)
        last = jnp.where(named, code, last)
    first = jnp.min(first.astype(jnp.float32), axis=0, keepdims=True)
    last = jnp.max(last.astype(jnp.float32), axis=0, keepdims=True)
    second = jnp.where(last > first, last, float(NONE))
    return jnp.where(lanes((1, slots)) < insts, first, second)


def pack_kernel(prefix_hbm, queries_hbm, out, heads, stage, flat, prefix, queries, sems):
    fetch_prefix = pltpu.make_async_copy(prefix_hbm, prefix, sems.at[0])
    fetch_queries = pltpu.make_async_copy(queries_hbm, queries, sems.at[1])
    fetch_prefix.start()
    fetch_queries.start()
    insts = stage.shape[0] // ROWS
    for r in range(CAP * GRP + 1, ROWS):
        stage[pl.ds(r, insts, stride=ROWS), :] = jnp.zeros((insts, HD), jnp.float32)
    fetch_prefix.wait()
    slots = CAP * insts
    codes = jnp.broadcast_to(slot_codes(prefix[...], insts), (slots, slots)).T.astype(jnp.int32)
    pick = ((codes >> 7) == lanes(codes.shape))[:, :GRP].astype(jnp.float32).astype(jnp.bfloat16)
    fetch_queries.wait()
    picked = dot(pick, queries[...], NN)
    lane = lanes((insts, HD))
    local = (codes & 7).astype(jnp.float32)
    ids = jnp.where(lane == 0, local[:insts], jnp.where(lane == 1, local[insts:], 0.0))
    for k in range(CAP):
        for g in range(GRP):
            part = picked[k * insts : (k + 1) * insts, g * HD : (g + 1) * HD]
            stage[pl.ds(k * GRP + g, insts, stride=ROWS), :] = part
    stage[pl.ds(CAP * GRP, insts, stride=ROWS), :] = ids
    out[...] = stage[...].astype(jnp.bfloat16)
    own = queries[...].astype(jnp.float32)
    for g in range(GRP):
        flat[pl.ds(g, own.shape[0], stride=GRP), :] = own[:, g * HD : (g + 1) * HD]
    heads[...] = flat[...].astype(jnp.bfloat16)


def pack(insts, prefix, queries):
    size = insts * ROWS
    flat = queries.shape[0] * GRP
    hbm = pl.BlockSpec(memory_space=pltpu.HBM)
    vmem = pl.BlockSpec(memory_space=pltpu.VMEM)
    return pl.pallas_call(
        pack_kernel,
        out_shape=[
            jax.ShapeDtypeStruct((size, HD), jnp.bfloat16),
            jax.ShapeDtypeStruct((flat, HD), jnp.bfloat16),
        ],
        in_specs=[hbm, hbm],
        out_specs=[vmem, vmem],
        scratch_shapes=[
            pltpu.VMEM((size, HD), jnp.float32),
            pltpu.VMEM((flat, HD), jnp.float32),
            pltpu.VMEM(prefix.shape, prefix.dtype),
            pltpu.VMEM(queries.shape, queries.dtype),
            pltpu.SemaphoreType.DMA((2,)),
        ],
        compiler_params=pltpu.CompilerParams(vmem_limit_bytes=8 * MIB),
        cost_estimate=pl.CostEstimate(flops=1 << 22, bytes_accessed=1 << 19, transcendentals=0),
        name="pack",
    )(in_hbm(prefix), in_hbm(queries))


def attend(queries, cache, slots, lengths):
    scores = [dot(q, cache[s, :, :HD], NT) * SCALE for q, s in zip(queries, slots)]
    valid = [lanes(x.shape) < jnp.broadcast_to(n, x.shape) for x, n in zip(scores, lengths)]
    peaks = [
        jnp.max(jnp.where(v, x, LOW), axis=1, keepdims=True) for x, v in zip(scores, valid)
    ]
    weights = [jnp.where(v, jnp.exp(x - p), 0.0) for x, v, p in zip(scores, valid, peaks)]
    mixes = [dot(w.astype(jnp.bfloat16), cache[s, :, HD:], NN) for w, s in zip(weights, slots)]
    totals = [jnp.sum(w, axis=1, keepdims=True) for w in weights]
    stats = [jnp.where(lanes((GRP, HD)) == 0, p, t) for p, t in zip(peaks, totals)]
    return mixes, stats


def prepare_kernel(mig, lengths, pool_hbm, cache_hbm, keys, values, leaving, pool, sems):
    tokens = cache_hbm.shape[1]
    fetch_pool = pltpu.make_async_copy(pool_hbm, pool, sems.at[0])
    fetch_row = pltpu.make_async_copy(
        cache_hbm.at[mig[0]], leaving.at[pl.ds(0, tokens)], sems.at[1]
    )
    fetch_pool.start()
    fetch_row.start()
    length = lengths[mig[0]]
    lane = lanes((TAIL, leaving.shape[1]))
    tail = jnp.where(lane == 0, length >> 3, jnp.where(lane == 1, length & 7, 0))
    leaving[tokens:] = tail.astype(jnp.float32).astype(jnp.bfloat16)
    fetch_pool.wait()
    half = pool.shape[0] // BLK // 2
    for p in range(half):
        for b in range(2):
            block = slice((2 * p + b) * BLK, (2 * p + b + 1) * BLK)
            keys[p * BLK : (p + 1) * BLK, b * HD : (b + 1) * HD] = pool[block, :HD]
    for b in range(2):
        part = slice(b * half * BLK, (b + 1) * half * BLK)
        values[:, b * HD : (b + 1) * HD] = pool[part, HD:]
    fetch_row.wait()


def prepare(mig, lengths, pool, cache):
    rows, tokens, width = cache.shape
    smem = pl.BlockSpec(memory_space=pltpu.SMEM)
    vmem = pl.BlockSpec(memory_space=pltpu.VMEM)
    hbm = pl.BlockSpec(memory_space=pltpu.HBM)
    paired = jax.ShapeDtypeStruct((pool.shape[0] // 2, 2 * HD), pool.dtype)
    return pl.pallas_call(
        prepare_kernel,
        out_shape=[paired, paired, jax.ShapeDtypeStruct((tokens + TAIL, width), cache.dtype)],
        in_specs=[smem, smem, hbm, hbm],
        out_specs=[vmem, vmem, vmem],
        scratch_shapes=[pltpu.VMEM(pool.shape, pool.dtype), pltpu.SemaphoreType.DMA((2,))],
        compiler_params=pltpu.CompilerParams(vmem_limit_bytes=8 * MIB),
        cost_estimate=pl.CostEstimate(
            flops=0, bytes_accessed=2 * (pool.size + tokens * width), transcendentals=0
        ),
        name="prepare",
    )(mig, lengths, in_hbm(pool), in_hbm(cache))


def resident_kernel(
    mig, lengths, query, new_kv_hbm, moved, cache_hbm, out, cache, tail, new_kv, sems, sem_tail, sem_new
):
    rows, tokens, _ = cache.shape
    fetch_tail = pltpu.make_async_copy(moved.at[pl.ds(tokens, TAIL)], tail, sem_tail)
    fetch_new = pltpu.make_async_copy(new_kv_hbm, new_kv, sem_new)
    fetch_tail.start()
    fetch_new.start()
    fetches = []
    for s in range(rows):
        here = pltpu.make_async_copy(cache_hbm.at[s], cache.at[s], sems.at[s])
        came = pltpu.make_async_copy(moved.at[pl.ds(0, tokens)], cache.at[s], sems.at[s])
        pl.when(mig[0] != s)(here.start)
        pl.when(mig[0] == s)(came.start)
        fetches.append(here)
    fetch_tail.wait()
    fetch_new.wait()
    parts = tail[...].astype(jnp.float32)
    moved_length = (parts[0:1, 0:1] * 8.0 + parts[0:1, 1:2]).astype(jnp.int32)
    length = [jnp.where(mig[0] == s, moved_length, lengths[s]) for s in range(rows)]
    key = new_kv[:, :HD].astype(jnp.float32)
    fresh = [
        jnp.sum(query[s].astype(jnp.float32) * key[s : s + 1], axis=1, keepdims=True) * SCALE
        for s in range(rows)
    ]
    for c in range(0, rows, TOGETHER):
        slots = range(c, c + TOGETHER)
        for s in slots:
            fetches[s].wait()
        mixes, stats = attend([query[s] for s in slots], cache, slots, [length[s] for s in slots])
        for s, mix, stat in zip(slots, mixes, stats):
            out[s, :GRP] = mix
            out[s, GRP:] = jnp.where(lanes((GRP, HD)) == 2, fresh[s], stat)


def resident(mig, lengths, query, new_kv, moved, cache):
    rows, tokens, width = cache.shape
    smem = pl.BlockSpec(memory_space=pltpu.SMEM)
    vmem = pl.BlockSpec(memory_space=pltpu.VMEM)
    hbm = pl.BlockSpec(memory_space=pltpu.HBM)
    return pl.pallas_call(
        resident_kernel,
        out_shape=jax.ShapeDtypeStruct((rows, 2 * GRP, HD), jnp.float32),
        in_specs=[smem, smem, vmem, hbm, pl.BlockSpec(memory_space=pl.ANY), hbm],
        out_specs=vmem,
        scratch_shapes=[
            pltpu.VMEM(cache.shape, cache.dtype),
            pltpu.VMEM((TAIL, width), cache.dtype),
            pltpu.VMEM(new_kv.shape, new_kv.dtype),
            pltpu.SemaphoreType.DMA((rows,)),
            pltpu.SemaphoreType.DMA,
            pltpu.SemaphoreType.DMA,
        ],
        compiler_params=pltpu.CompilerParams(vmem_limit_bytes=12 * MIB),
        cost_estimate=pl.CostEstimate(
            flops=1 << 34, bytes_accessed=1 << 26, transcendentals=rows * GRP * tokens
        ),
        name="resident",
    )(mig, lengths, query, in_hbm(new_kv), moved, in_hbm(cache))


def owner_kernel(arrived, keys, values, out, stage):
    stage[...] = arrived[...].astype(jnp.float32)
    insts = stage.shape[0] // ROWS
    slots = CAP * insts
    half = keys.shape[0] // BLK

    def rows_of(r):
        return stage[pl.ds(r, insts, stride=ROWS), :]

    ids = rows_of(CAP * GRP)
    local = jnp.concatenate([ids[:, k : k + 1] for k in range(CAP)], axis=0).astype(jnp.int32)
    local = jnp.broadcast_to(local, (slots, BLK))
    odd = (local & 1) == 1
    pair = jnp.concatenate([local >> 1] * HEADS, axis=0)
    rest = jnp.concatenate([local & (half - 1)] * HEADS, axis=0)
    upper = jnp.concatenate([local >= half] * HEADS, axis=0)
    lane = lanes((slots, HD))

    def score(c):
        query = []
        for g in range(c * HEADS, (c + 1) * HEADS):
            part = jnp.concatenate([rows_of(k * GRP + g) for k in range(CAP)], axis=0)
            halves = [jnp.where(odd, 0.0, part), jnp.where(odd, part, 0.0)]
            query.append(jnp.concatenate(halves, axis=1).astype(jnp.bfloat16))
        return dot(jnp.concatenate(query, axis=0), keys[...], NT)

    def weigh(scores):
        picked = scores[:, :BLK]
        for p in range(1, half):
            picked = jnp.where(pair == p, scores[:, p * BLK : (p + 1) * BLK], picked)
        picked = picked * SCALE
        peak = jnp.max(picked, axis=1, keepdims=True).astype(jnp.bfloat16).astype(jnp.float32)
        weights = jnp.exp(picked - peak)
        total = jnp.sum(weights, axis=1, keepdims=True)
        spread = [jnp.where(rest == b, weights, 0.0).astype(jnp.bfloat16) for b in range(half)]
        return jnp.concatenate(spread, axis=1), peak, total

    def mix(spread):
        both = dot(spread, values[...], NN)
        return jnp.where(upper, both[:, HD:], both[:, :HD])

    chunks = GRP // HEADS
    stats = jnp.zeros((slots, HD), jnp.float32)
    mixes = []
    scores = score(0)
    waiting = None
    for c in range(chunks):
        following = score(c + 1) if c + 1 < chunks else None
        spread, peak, total = weigh(scores)
        if waiting is not None:
            mixes.append(mix(waiting))
        total_hi = total.astype(jnp.bfloat16).astype(jnp.float32)
        total_lo = total - total_hi
        for h in range(HEADS):
            g = c * HEADS + h
            part = slice(h * slots, (h + 1) * slots)
            stats = jnp.where(lane == g, peak[part], stats)
            stats = jnp.where(lane == GRP + g, total_hi[part], stats)
            stats = jnp.where(lane == 2 * GRP + g, total_lo[part], stats)
        scores, waiting = following, spread
    mixes.append(mix(waiting))
    for k in range(CAP):
        for g in range(GRP):
            start = g % HEADS * slots + k * insts
            part = mixes[g // HEADS][start : start + insts]
            stage[pl.ds(k * GRP + g, insts, stride=ROWS), :] = part
        stage[pl.ds(CAP * GRP + k, insts, stride=ROWS), :] = stats[k * insts : (k + 1) * insts]
    out[...] = stage[...].astype(jnp.bfloat16)


def owner(arrived, keys, values):
    vmem = pl.BlockSpec(memory_space=pltpu.VMEM)
    return pl.pallas_call(
        owner_kernel,
        out_shape=jax.ShapeDtypeStruct(arrived.shape, jnp.bfloat16),
        in_specs=[vmem, vmem, vmem],
        out_specs=vmem,
        scratch_shapes=[pltpu.VMEM(arrived.shape, jnp.float32)],
        compiler_params=pltpu.CompilerParams(vmem_limit_bytes=24 * MIB),
        cost_estimate=pl.CostEstimate(
            flops=1 << 29, bytes_accessed=2 << 20, transcendentals=1 << 17
        ),
        name="owner",
    )(arrived, keys, values)


def combine_kernel(prefix, arrived, own, new_kv, out, wide, table):
    wide[...] = arrived[...].astype(jnp.float32)
    insts = wide.shape[0] // ROWS
    rows = own.shape[0]
    slots = CAP * insts
    codes = slot_codes(prefix[...], insts).astype(jnp.int32)
    belongs = jnp.where(codes < NONE, codes >> 7, -1)

    def rows_of(r):
        return wide[pl.ds(r, insts, stride=ROWS), :]

    stats = jnp.concatenate([rows_of(CAP * GRP + k) for k in range(CAP)], axis=0).T
    peak = stats[:GRP]
    total = stats[GRP : 2 * GRP] + stats[2 * GRP : 3 * GRP]
    values = new_kv[:, HD:].astype(jnp.float32)
    below, mixes = [], []
    for s in range(rows):
        mine = jnp.broadcast_to(belongs, (GRP, slots)) == s
        stat = own[s, GRP:]
        res_peak, res_total, new_peak = stat[:, 0:1], stat[:, 1:2], stat[:, 2:3]
        top = jnp.max(jnp.where(mine, peak, LOW), axis=1, keepdims=True)
        top = jnp.maximum(jnp.maximum(top, res_peak), new_peak)
        weight = jnp.where(mine, jnp.exp(jnp.where(mine, peak, LOW) - top), 0.0)
        table[s * GRP : (s + 1) * GRP, :] = weight
        res_scale = jnp.exp(res_peak - top)
        new_scale = jnp.exp(new_peak - top)
        below.append(
            jnp.sum(weight * total, axis=1, keepdims=True) + res_scale * res_total + new_scale
        )
        mixes.append(
            res_scale * own[s, :GRP] + new_scale * values[s : s + 1]
        )
    sums = []
    for g in range(GRP):
        weight = table[pl.ds(g, rows, stride=GRP), :]
        weight_hi = weight.astype(jnp.bfloat16).astype(jnp.float32)
        both = jnp.concatenate([weight_hi, weight - weight_hi], axis=0).astype(jnp.bfloat16)
        mix = jnp.concatenate([rows_of(k * GRP + g) for k in range(CAP)], axis=0)
        got = dot(both, mix.astype(jnp.bfloat16), NN)
        sums.append(got[:rows] + got[rows:])
    for g in range(GRP):
        table[pl.ds(g, rows, stride=GRP), :] = sums[g]
    attended = [
        (table[s * GRP : (s + 1) * GRP, :] + mixes[s]) / below[s]
        for s in (r ^ FIRST_TP for r in range(rows))
    ]
    out[...] = jnp.concatenate(attended, axis=0).astype(jnp.bfloat16)


def combine(prefix, arrived, own, new_kv):
    rows = own.shape[0]
    vmem = pl.BlockSpec(memory_space=pltpu.VMEM)
    return pl.pallas_call(
        combine_kernel,
        out_shape=jax.ShapeDtypeStruct((rows * GRP, HD), jnp.bfloat16),
        in_specs=[vmem] * 4,
        out_specs=vmem,
        scratch_shapes=[
            pltpu.VMEM(arrived.shape, jnp.float32),
            pltpu.VMEM((rows * GRP, HD), jnp.float32),
        ],
        compiler_params=pltpu.CompilerParams(vmem_limit_bytes=8 * MIB),
        cost_estimate=pl.CostEstimate(flops=1 << 24, bytes_accessed=1 << 20, transcendentals=8192),
        name="combine",
    )(prefix, arrived, own, new_kv)


def on_device(queries, new_kv, cache, lengths, migrate_slot, pool, prefix_blocks):
    rows = queries.shape[0]
    insts = lax.axis_size("inst")
    swap = [(i, i ^ (insts // 2)) for i in range(insts)]
    order = [[r ^ FIRST for r in range(insts)]]
    order_tp = [[r ^ FIRST_TP for r in range(rows)]]

    def exchange(messages):
        messages = messages.reshape(insts, ROWS // 2, 2, HD)
        arrived = lax.all_to_all(
            messages, "inst", split_axis=0, concat_axis=0, axis_index_groups=order, tiled=True
        )
        return arrived.reshape(-1, HD)

    messages, query = pack(insts, prefix_blocks, queries)
    asked = exchange(messages)
    keys, values, leaving = prepare(migrate_slot, lengths, pool.reshape(-1, 2 * HD), cache)
    moved = lax.ppermute(leaving, "inst", swap)
    answers = exchange(owner(asked, keys, values))
    query = query.reshape(rows, GRP, HD)
    own = resident(migrate_slot, lengths, query, new_kv, moved, cache)
    attended = combine(prefix_blocks, answers, own, new_kv)
    attended = attended.reshape(rows, GRP, HD)
    heads = lax.all_to_all(
        attended, "tp", split_axis=0, concat_axis=0, axis_index_groups=order_tp, tiled=True
    )
    heads = jnp.concatenate([heads[FIRST_TP:], heads[:FIRST_TP]], axis=0)
    return heads.reshape(1, -1)


def solution(mesh):
    in_specs = (
        P("inst", "tp"),
        P("inst", "tp"),
        P("inst", None, "tp"),
        P("inst"),
        P("inst"),
        P("inst", None, "tp"),
        P("inst", None),
    )
    out_specs = P(("inst", "tp"), None)
    return jax.shard_map(
        on_device, mesh=mesh, in_specs=in_specs, out_specs=out_specs, check_vma=False
    )
```

```python
import jax
import jax.numpy as jnp
from jax import lax
from jax.experimental import pallas as pl
from jax.experimental.pallas import tpu as pltpu
from jax.sharding import PartitionSpec as P

QH = 64
KVH = 8
HD = 128
BLK = 128
GRP = QH // KVH
CAP = 2
NONE = 8191
FIRST = 22
FIRST_TP = 4
TAIL = 16
HEADS = 2
TOGETHER = 4
ROWS = 18
SCALE = HD**-0.5
LOW = -1e30
MIB = 1024 * 1024

NT = (((1,), (1,)), ((), ()))
NN = (((1,), (0,)), ((), ()))


def dot(a, b, dims):
    return lax.dot_general(a, b, dims, preferred_element_type=jnp.float32)


def in_hbm(x):
    return pltpu.with_memory_space_constraint(x, pltpu.HBM)


def lanes(shape):
    return lax.broadcasted_iota(jnp.int32, shape, len(shape) - 1)


def slot_codes(ids, insts):
    rows, width = ids.shape
    slots = CAP * insts
    lane = (lanes((rows, slots)) & (insts - 1)) ^ FIRST
    row = lax.broadcasted_iota(jnp.int32, (rows, slots), 0)
    first = jnp.full((rows, slots), NONE, jnp.int32)
    last = jnp.full((rows, slots), -1, jnp.int32)
    for e in range(width):
        entry = jnp.broadcast_to(ids[:, e : e + 1], (rows, slots))
        named = (entry >= 0) & ((entry >> 3) == lane)
        code = (row * width + e) * 8 + (entry & 7)
        first = jnp.where(named, jnp.minimum(first, code), first)
        last = jnp.where(named, code, last)
    first = jnp.min(first.astype(jnp.float32), axis=0, keepdims=True)
    last = jnp.max(last.astype(jnp.float32), axis=0, keepdims=True)
    second = jnp.where(last > first, last, float(NONE))
    return jnp.where(lanes((1, slots)) < insts, first, second)


def pack_kernel(prefix_hbm, queries_hbm, out, heads, stage, flat, prefix, queries, sems):
    fetch_prefix = pltpu.make_async_copy(prefix_hbm, prefix, sems.at[0])
    fetch_queries = pltpu.make_async_copy(queries_hbm, queries, sems.at[1])
    fetch_prefix.start()
    fetch_queries.start()
    insts = stage.shape[0] // ROWS
    for r in range(CAP * GRP + 1, ROWS):
        stage[pl.ds(r, insts, stride=ROWS), :] = jnp.zeros((insts, HD), jnp.float32)
    fetch_prefix.wait()
    slots = CAP * insts
    codes = jnp.broadcast_to(slot_codes(prefix[...], insts), (slots, slots)).T.astype(jnp.int32)
    pick = ((codes >> 7) == lanes(codes.shape))[:, :GRP].astype(jnp.float32).astype(jnp.bfloat16)
    fetch_queries.wait()
    picked = dot(pick, queries[...], NN)
    lane = lanes((insts, HD))
    local = (codes & 7).astype(jnp.float32)
    ids = jnp.where(lane == 0, local[:insts], jnp.where(lane == 1, local[insts:], 0.0))
    for k in range(CAP):
        for g in range(GRP):
            part = picked[k * insts : (k + 1) * insts, g * HD : (g + 1) * HD]
            stage[pl.ds(k * GRP + g, insts, stride=ROWS), :] = part
    stage[pl.ds(CAP * GRP, insts, stride=ROWS), :] = ids
    out[...] = stage[...].astype(jnp.bfloat16)
    own = queries[...].astype(jnp.float32)
    for g in range(GRP):
        flat[pl.ds(g, own.shape[0], stride=GRP), :] = own[:, g * HD : (g + 1) * HD]
    heads[...] = flat[...].astype(jnp.bfloat16)


def pack(insts, prefix, queries):
    size = insts * ROWS
    flat = queries.shape[0] * GRP
    hbm = pl.BlockSpec(memory_space=pltpu.HBM)
    vmem = pl.BlockSpec(memory_space=pltpu.VMEM)
    return pl.pallas_call(
        pack_kernel,
        out_shape=[
            jax.ShapeDtypeStruct((size, HD), jnp.bfloat16),
            jax.ShapeDtypeStruct((flat, HD), jnp.bfloat16),
        ],
        in_specs=[hbm, hbm],
        out_specs=[vmem, vmem],
        scratch_shapes=[
            pltpu.VMEM((size, HD), jnp.float32),
            pltpu.VMEM((flat, HD), jnp.float32),
            pltpu.VMEM(prefix.shape, prefix.dtype),
            pltpu.VMEM(queries.shape, queries.dtype),
            pltpu.SemaphoreType.DMA((2,)),
        ],
        compiler_params=pltpu.CompilerParams(vmem_limit_bytes=8 * MIB),
        cost_estimate=pl.CostEstimate(flops=1 << 22, bytes_accessed=1 << 19, transcendentals=0),
        name="pack",
    )(in_hbm(prefix), in_hbm(queries))


def attend(queries, cache, slots, lengths):
    scores = [dot(q, cache[s, :, :HD], NT) * SCALE for q, s in zip(queries, slots)]
    valid = [lanes(x.shape) < jnp.broadcast_to(n, x.shape) for x, n in zip(scores, lengths)]
    peaks = [
        jnp.max(jnp.where(v, x, LOW), axis=1, keepdims=True) for x, v in zip(scores, valid)
    ]
    weights = [jnp.where(v, jnp.exp(x - p), 0.0) for x, v, p in zip(scores, valid, peaks)]
    mixes = [dot(w.astype(jnp.bfloat16), cache[s, :, HD:], NN) for w, s in zip(weights, slots)]
    totals = [jnp.sum(w, axis=1, keepdims=True) for w in weights]
    stats = [jnp.where(lanes((GRP, HD)) == 0, p, t) for p, t in zip(peaks, totals)]
    return mixes, stats


def prepare_kernel(mig, lengths_hbm, pool, cache, keys, values, leaving, lengths, sems):
    tokens = cache.shape[1]
    fetches = [
        (cache.at[mig[0]], leaving.at[pl.ds(0, tokens)]),
        (lengths_hbm, lengths),
    ]
    half = keys.shape[0] // BLK
    for b in range(2):
        lanes_of = pl.ds(b * HD, HD)
        part = pl.ds(b * half * BLK, half * BLK)
        fetches.append((pool.at[part, pl.ds(HD, HD)], values.at[:, lanes_of]))
        for p in range(half):
            block = pl.ds((2 * p + b) * BLK, BLK)
            fetches.append((pool.at[block, pl.ds(0, HD)], keys.at[pl.ds(p * BLK, BLK), lanes_of]))
    fetches = [pltpu.make_async_copy(*ends, sems.at[n]) for n, ends in enumerate(fetches)]
    for fetch in fetches:
        fetch.start()
    fetches[1].wait()
    length = lengths[mig[0]]
    lane = lanes((TAIL, leaving.shape[1]))
    tail = jnp.where(lane == 0, length >> 3, jnp.where(lane == 1, length & 7, 0))
    leaving[tokens:] = tail.astype(jnp.float32).astype(jnp.bfloat16)
    fetches[0].wait()
    for fetch in fetches[2:]:
        fetch.wait()


def prepare(mig, lengths, pool, cache):
    rows, tokens, width = cache.shape
    smem = pl.BlockSpec(memory_space=pltpu.SMEM)
    vmem = pl.BlockSpec(memory_space=pltpu.VMEM)
    hbm = pl.BlockSpec(memory_space=pltpu.HBM)
    paired = jax.ShapeDtypeStruct((pool.shape[0] // 2, 2 * HD), pool.dtype)
    return pl.pallas_call(
        prepare_kernel,
        out_shape=[paired, paired, jax.ShapeDtypeStruct((tokens + TAIL, width), cache.dtype)],
        in_specs=[smem, hbm, hbm, hbm],
        out_specs=[vmem, vmem, vmem],
        scratch_shapes=[
            pltpu.SMEM(lengths.shape, lengths.dtype),
            pltpu.SemaphoreType.DMA((4 + pool.shape[0] // BLK,)),
        ],
        compiler_params=pltpu.CompilerParams(vmem_limit_bytes=8 * MIB),
        cost_estimate=pl.CostEstimate(
            flops=0, bytes_accessed=2 * (pool.size + tokens * width), transcendentals=0
        ),
        name="prepare",
    )(mig, in_hbm(lengths), in_hbm(pool), in_hbm(cache))


def resident_kernel(
    mig, lengths, query, new_kv_hbm, moved, cache_hbm, out, cache, tail, new_kv, sems, sem_tail, sem_new
):
    rows, tokens, _ = cache.shape
    fetch_tail = pltpu.make_async_copy(moved.at[pl.ds(tokens, TAIL)], tail, sem_tail)
    fetch_new = pltpu.make_async_copy(new_kv_hbm, new_kv, sem_new)
    fetch_tail.start()
    fetch_new.start()
    fetches = []
    for s in range(rows):
        here = pltpu.make_async_copy(cache_hbm.at[s], cache.at[s], sems.at[s])
        came = pltpu.make_async_copy(moved.at[pl.ds(0, tokens)], cache.at[s], sems.at[s])
        pl.when(mig[0] != s)(here.start)
        pl.when(mig[0] == s)(came.start)
        fetches.append(here)
    fetch_tail.wait()
    fetch_new.wait()
    parts = tail[...].astype(jnp.float32)
    moved_length = (parts[0:1, 0:1] * 8.0 + parts[0:1, 1:2]).astype(jnp.int32)
    length = [jnp.where(mig[0] == s, moved_length, lengths[s]) for s in range(rows)]
    key = new_kv[:, :HD].astype(jnp.float32)
    fresh = [
        jnp.sum(query[s].astype(jnp.float32) * key[s : s + 1], axis=1, keepdims=True) * SCALE
        for s in range(rows)
    ]
    for c in range(0, rows, TOGETHER):
        slots = range(c, c + TOGETHER)
        for s in slots:
            fetches[s].wait()
        mixes, stats = attend([query[s] for s in slots], cache, slots, [length[s] for s in slots])
        for s, mix, stat in zip(slots, mixes, stats):
            out[s, :GRP] = mix
            out[s, GRP:] = jnp.where(lanes((GRP, HD)) == 2, fresh[s], stat)


def resident(mig, lengths, query, new_kv, moved, cache):
    rows, tokens, width = cache.shape
    smem = pl.BlockSpec(memory_space=pltpu.SMEM)
    vmem = pl.BlockSpec(memory_space=pltpu.VMEM)
    hbm = pl.BlockSpec(memory_space=pltpu.HBM)
    return pl.pallas_call(
        resident_kernel,
        out_shape=jax.ShapeDtypeStruct((rows, 2 * GRP, HD), jnp.float32),
        in_specs=[smem, smem, vmem, hbm, pl.BlockSpec(memory_space=pl.ANY), hbm],
        out_specs=vmem,
        scratch_shapes=[
            pltpu.VMEM(cache.shape, cache.dtype),
            pltpu.VMEM((TAIL, width), cache.dtype),
            pltpu.VMEM(new_kv.shape, new_kv.dtype),
            pltpu.SemaphoreType.DMA((rows,)),
            pltpu.SemaphoreType.DMA,
            pltpu.SemaphoreType.DMA,
        ],
        compiler_params=pltpu.CompilerParams(vmem_limit_bytes=12 * MIB),
        cost_estimate=pl.CostEstimate(
            flops=1 << 34, bytes_accessed=1 << 26, transcendentals=rows * GRP * tokens
        ),
        name="resident",
    )(mig, lengths, query, in_hbm(new_kv), moved, in_hbm(cache))


def owner_kernel(arrived, keys, values, out, stage):
    stage[...] = arrived[...].astype(jnp.float32)
    insts = stage.shape[0] // ROWS
    slots = CAP * insts
    half = keys.shape[0] // BLK

    def rows_of(r):
        return stage[pl.ds(r, insts, stride=ROWS), :]

    ids = rows_of(CAP * GRP)
    local = jnp.concatenate([ids[:, k : k + 1] for k in range(CAP)], axis=0).astype(jnp.int32)
    local = jnp.broadcast_to(local, (slots, BLK))
    odd = (local & 1) == 1
    pair = jnp.concatenate([local >> 1] * HEADS, axis=0)
    rest = jnp.concatenate([local & (half - 1)] * HEADS, axis=0)
    upper = jnp.concatenate([local >= half] * HEADS, axis=0)
    lane = lanes((slots, HD))

    def score(c):
        query = []
        for g in range(c * HEADS, (c + 1) * HEADS):
            part = jnp.concatenate([rows_of(k * GRP + g) for k in range(CAP)], axis=0)
            halves = [jnp.where(odd, 0.0, part), jnp.where(odd, part, 0.0)]
            query.append(jnp.concatenate(halves, axis=1).astype(jnp.bfloat16))
        return dot(jnp.concatenate(query, axis=0), keys[...], NT)

    def weigh(scores):
        picked = scores[:, :BLK]
        for p in range(1, half):
            picked = jnp.where(pair == p, scores[:, p * BLK : (p + 1) * BLK], picked)
        picked = picked * SCALE
        peak = jnp.max(picked, axis=1, keepdims=True).astype(jnp.bfloat16).astype(jnp.float32)
        weights = jnp.exp(picked - peak)
        total = jnp.sum(weights, axis=1, keepdims=True)
        spread = [jnp.where(rest == b, weights, 0.0).astype(jnp.bfloat16) for b in range(half)]
        return jnp.concatenate(spread, axis=1), peak, total

    def mix(spread):
        both = dot(spread, values[...], NN)
        return jnp.where(upper, both[:, HD:], both[:, :HD])

    chunks = GRP // HEADS
    stats = jnp.zeros((slots, HD), jnp.float32)
    mixes = []
    scores = score(0)
    waiting = None
    for c in range(chunks):
        following = score(c + 1) if c + 1 < chunks else None
        spread, peak, total = weigh(scores)
        if waiting is not None:
            mixes.append(mix(waiting))
        total_hi = total.astype(jnp.bfloat16).astype(jnp.float32)
        total_lo = total - total_hi
        for h in range(HEADS):
            g = c * HEADS + h
            part = slice(h * slots, (h + 1) * slots)
            stats = jnp.where(lane == g, peak[part], stats)
            stats = jnp.where(lane == GRP + g, total_hi[part], stats)
            stats = jnp.where(lane == 2 * GRP + g, total_lo[part], stats)
        scores, waiting = following, spread
    mixes.append(mix(waiting))
    for k in range(CAP):
        for g in range(GRP):
            start = g % HEADS * slots + k * insts
            part = mixes[g // HEADS][start : start + insts]
            stage[pl.ds(k * GRP + g, insts, stride=ROWS), :] = part
        stage[pl.ds(CAP * GRP + k, insts, stride=ROWS), :] = stats[k * insts : (k + 1) * insts]
    out[...] = stage[...].astype(jnp.bfloat16)


def owner(arrived, keys, values):
    vmem = pl.BlockSpec(memory_space=pltpu.VMEM)
    return pl.pallas_call(
        owner_kernel,
        out_shape=jax.ShapeDtypeStruct(arrived.shape, jnp.bfloat16),
        in_specs=[vmem, vmem, vmem],
        out_specs=vmem,
        scratch_shapes=[pltpu.VMEM(arrived.shape, jnp.float32)],
        compiler_params=pltpu.CompilerParams(vmem_limit_bytes=24 * MIB),
        cost_estimate=pl.CostEstimate(
            flops=1 << 29, bytes_accessed=2 << 20, transcendentals=1 << 17
        ),
        name="owner",
    )(arrived, keys, values)


def combine_kernel(prefix, arrived, own, new_kv, out, wide, table):
    wide[...] = arrived[...].astype(jnp.float32)
    insts = wide.shape[0] // ROWS
    rows = own.shape[0]
    slots = CAP * insts
    codes = slot_codes(prefix[...], insts).astype(jnp.int32)
    belongs = jnp.where(codes < NONE, codes >> 7, -1)

    def rows_of(r):
        return wide[pl.ds(r, insts, stride=ROWS), :]

    stats = jnp.concatenate([rows_of(CAP * GRP + k) for k in range(CAP)], axis=0).T
    peak = stats[:GRP]
    total = stats[GRP : 2 * GRP] + stats[2 * GRP : 3 * GRP]
    values = new_kv[:, HD:].astype(jnp.float32)
    below, mixes = [], []
    for s in range(rows):
        mine = jnp.broadcast_to(belongs, (GRP, slots)) == s
        stat = own[s, GRP:]
        res_peak, res_total, new_peak = stat[:, 0:1], stat[:, 1:2], stat[:, 2:3]
        top = jnp.max(jnp.where(mine, peak, LOW), axis=1, keepdims=True)
        top = jnp.maximum(jnp.maximum(top, res_peak), new_peak)
        weight = jnp.where(mine, jnp.exp(jnp.where(mine, peak, LOW) - top), 0.0)
        table[s * GRP : (s + 1) * GRP, :] = weight
        res_scale = jnp.exp(res_peak - top)
        new_scale = jnp.exp(new_peak - top)
        below.append(
            jnp.sum(weight * total, axis=1, keepdims=True) + res_scale * res_total + new_scale
        )
        mixes.append(
            res_scale * own[s, :GRP] + new_scale * values[s : s + 1]
        )
    sums = []
    for g in range(GRP):
        weight = table[pl.ds(g, rows, stride=GRP), :]
        weight_hi = weight.astype(jnp.bfloat16).astype(jnp.float32)
        both = jnp.concatenate([weight_hi, weight - weight_hi], axis=0).astype(jnp.bfloat16)
        mix = jnp.concatenate([rows_of(k * GRP + g) for k in range(CAP)], axis=0)
        got = dot(both, mix.astype(jnp.bfloat16), NN)
        sums.append(got[:rows] + got[rows:])
    for g in range(GRP):
        table[pl.ds(g, rows, stride=GRP), :] = sums[g]
    attended = [
        (table[s * GRP : (s + 1) * GRP, :] + mixes[s]) / below[s]
        for s in (r ^ FIRST_TP for r in range(rows))
    ]
    out[...] = jnp.concatenate(attended, axis=0).astype(jnp.bfloat16)


def combine(prefix, arrived, own, new_kv):
    rows = own.shape[0]
    vmem = pl.BlockSpec(memory_space=pltpu.VMEM)
    return pl.pallas_call(
        combine_kernel,
        out_shape=jax.ShapeDtypeStruct((rows * GRP, HD), jnp.bfloat16),
        in_specs=[vmem] * 4,
        out_specs=vmem,
        scratch_shapes=[
            pltpu.VMEM(arrived.shape, jnp.float32),
            pltpu.VMEM((rows * GRP, HD), jnp.float32),
        ],
        compiler_params=pltpu.CompilerParams(vmem_limit_bytes=8 * MIB),
        cost_estimate=pl.CostEstimate(flops=1 << 24, bytes_accessed=1 << 20, transcendentals=8192),
        name="combine",
    )(prefix, arrived, own, new_kv)


def on_device(queries, new_kv, cache, lengths, migrate_slot, pool, prefix_blocks):
    rows = queries.shape[0]
    insts = lax.axis_size("inst")
    swap = [(i, i ^ (insts // 2)) for i in range(insts)]
    order = [[r ^ FIRST for r in range(insts)]]
    order_tp = [[r ^ FIRST_TP for r in range(rows)]]

    def exchange(messages):
        messages = messages.reshape(insts, ROWS // 2, 2, HD)
        arrived = lax.all_to_all(
            messages, "inst", split_axis=0, concat_axis=0, axis_index_groups=order, tiled=True
        )
        return arrived.reshape(-1, HD)

    messages, query = pack(insts, prefix_blocks, queries)
    asked = exchange(messages)
    keys, values, leaving = prepare(migrate_slot, lengths, pool.reshape(-1, 2 * HD), cache)
    moved = lax.ppermute(leaving, "inst", swap)
    answers = exchange(owner(asked, keys, values))
    query = query.reshape(rows, GRP, HD)
    own = resident(migrate_slot, lengths, query, new_kv, moved, cache)
    attended = combine(prefix_blocks, answers, own, new_kv)
    attended = attended.reshape(rows, GRP, HD)
    heads = lax.all_to_all(
        attended, "tp", split_axis=0, concat_axis=0, axis_index_groups=order_tp, tiled=True
    )
    heads = jnp.concatenate([heads[FIRST_TP:], heads[:FIRST_TP]], axis=0)
    return heads.reshape(1, -1)


def solution(mesh):
    in_specs = (
        P("inst", "tp"),
        P("inst", "tp"),
        P("inst", None, "tp"),
        P("inst"),
        P("inst"),
        P("inst", None, "tp"),
        P("inst", None),
    )
    out_specs = P(("inst", "tp"), None)
    return jax.shard_map(
        on_device, mesh=mesh, in_specs=in_specs, out_specs=out_specs, check_vma=False
    )
```

```python
import jax
import jax.numpy as jnp
from jax import lax
from jax.experimental import pallas as pl
from jax.experimental.pallas import tpu as pltpu
from jax.sharding import PartitionSpec as P

QH = 64
KVH = 8
HD = 128
BLK = 128
GRP = QH // KVH
CAP = 2
NONE = 8191
FIRST = 20
FIRST_TP = 4
TAIL = 16
HEADS = 2
TOGETHER = 4
ROWS = 18
SCALE = HD**-0.5
LOW = -1e30
MIB = 1024 * 1024

NT = (((1,), (1,)), ((), ()))
NN = (((1,), (0,)), ((), ()))


def dot(a, b, dims):
    return lax.dot_general(a, b, dims, preferred_element_type=jnp.float32)


def in_hbm(x):
    return pltpu.with_memory_space_constraint(x, pltpu.HBM)


def lanes(shape):
    return lax.broadcasted_iota(jnp.int32, shape, len(shape) - 1)


def slot_codes(ids, insts):
    rows, width = ids.shape
    slots = CAP * insts
    lane = (lanes((rows, slots)) & (insts - 1)) ^ FIRST
    row = lax.broadcasted_iota(jnp.int32, (rows, slots), 0)
    first = jnp.full((rows, slots), NONE, jnp.int32)
    last = jnp.full((rows, slots), -1, jnp.int32)
    for e in range(width):
        entry = jnp.broadcast_to(ids[:, e : e + 1], (rows, slots))
        named = (entry >= 0) & ((entry >> 3) == lane)
        code = (row * width + e) * 8 + (entry & 7)
        first = jnp.where(named, jnp.minimum(first, code), first)
        last = jnp.where(named, code, last)
    first = jnp.min(first.astype(jnp.float32), axis=0, keepdims=True)
    last = jnp.max(last.astype(jnp.float32), axis=0, keepdims=True)
    second = jnp.where(last > first, last, float(NONE))
    return jnp.where(lanes((1, slots)) < insts, first, second)


def send_out(put, insts, stage, packed, out, sems):
    half = insts // 2
    copies = []
    for h in range(2):
        for r, part in put:
            first = h * half * ROWS + r
            stage[pl.ds(first, half, stride=ROWS), :] = part[h * half : (h + 1) * half]
        span = pl.ds(h * half * ROWS, half * ROWS)
        packed[span, :] = stage[span, :].astype(jnp.bfloat16)
        copies.append(pltpu.make_async_copy(packed.at[span], out.at[span], sems.at[h]))
        copies[h].start()
    for copy in copies:
        copy.wait()


def pack_kernel(prefix_hbm, queries_hbm, out, stage, packed, prefix, queries, sems, out_sems):
    fetch_prefix = pltpu.make_async_copy(prefix_hbm, prefix, sems.at[0])
    fetch_queries = pltpu.make_async_copy(queries_hbm, queries, sems.at[1])
    fetch_prefix.start()
    fetch_queries.start()
    insts = stage.shape[0] // ROWS
    slots = CAP * insts
    fetch_prefix.wait()
    codes = jnp.broadcast_to(slot_codes(prefix[...], insts), (slots, slots)).T.astype(jnp.int32)
    pick = ((codes >> 7) == lanes(codes.shape))[:, :GRP].astype(jnp.float32).astype(jnp.bfloat16)
    fetch_queries.wait()
    picked = dot(pick, queries[...], NN)
    lane = lanes((insts, HD))
    local = (codes & 7).astype(jnp.float32)
    ids = jnp.where(lane == 0, local[:insts], jnp.where(lane == 1, local[insts:], 0.0))
    put = [
        (k * GRP + g, picked[k * insts : (k + 1) * insts, g * HD : (g + 1) * HD])
        for k in range(CAP)
        for g in range(GRP)
    ]
    put.append((CAP * GRP, ids))
    put.append((CAP * GRP + 1, jnp.zeros((insts, HD), jnp.float32)))
    send_out(put, insts, stage, packed, out, out_sems)


def pack(insts, prefix, queries):
    size = insts * ROWS
    hbm = pl.BlockSpec(memory_space=pltpu.HBM)
    return pl.pallas_call(
        pack_kernel,
        out_shape=jax.ShapeDtypeStruct((size, HD), jnp.bfloat16),
        in_specs=[hbm, hbm],
        out_specs=pl.BlockSpec(memory_space=pl.ANY),
        scratch_shapes=[
            pltpu.VMEM((size, HD), jnp.float32),
            pltpu.VMEM((size, HD), jnp.bfloat16),
            pltpu.VMEM(prefix.shape, prefix.dtype),
            pltpu.VMEM(queries.shape, queries.dtype),
            pltpu.SemaphoreType.DMA((2,)),
            pltpu.SemaphoreType.DMA((2,)),
        ],
        compiler_params=pltpu.CompilerParams(vmem_limit_bytes=8 * MIB),
        cost_estimate=pl.CostEstimate(flops=1 << 22, bytes_accessed=1 << 19, transcendentals=0),
        name="pack",
    )(in_hbm(prefix), in_hbm(queries))


def attend(queries, cache, slots, lengths):
    scores = [dot(q, cache[s, :, :HD], NT) * SCALE for q, s in zip(queries, slots)]
    valid = [lanes(x.shape) < jnp.broadcast_to(n, x.shape) for x, n in zip(scores, lengths)]
    peaks = [
        jnp.max(jnp.where(v, x, LOW), axis=1, keepdims=True) for x, v in zip(scores, valid)
    ]
    weights = [jnp.where(v, jnp.exp(x - p), 0.0) for x, v, p in zip(scores, valid, peaks)]
    mixes = [dot(w.astype(jnp.bfloat16), cache[s, :, HD:], NN) for w, s in zip(weights, slots)]
    totals = [jnp.sum(w, axis=1, keepdims=True) for w in weights]
    stats = [jnp.where(lanes((GRP, HD)) == 0, p, t) for p, t in zip(peaks, totals)]
    return mixes, stats


def prepare_kernel(mig, lengths_hbm, pool, cache, keys, values, leaving, lengths, sems):
    tokens = cache.shape[1]
    fetches = [
        (cache.at[mig[0]], leaving.at[pl.ds(0, tokens)]),
        (lengths_hbm, lengths),
    ]
    half = keys.shape[0] // BLK
    for b in range(2):
        lanes_of = pl.ds(b * HD, HD)
        part = pl.ds(b * half * BLK, half * BLK)
        fetches.append((pool.at[part, pl.ds(HD, HD)], values.at[:, lanes_of]))
        for p in range(half):
            block = pl.ds((2 * p + b) * BLK, BLK)
            fetches.append((pool.at[block, pl.ds(0, HD)], keys.at[pl.ds(p * BLK, BLK), lanes_of]))
    fetches = [pltpu.make_async_copy(*ends, sems.at[n]) for n, ends in enumerate(fetches)]
    for fetch in fetches:
        fetch.start()
    fetches[1].wait()
    length = lengths[mig[0]]
    lane = lanes((TAIL, leaving.shape[1]))
    tail = jnp.where(lane == 0, length >> 3, jnp.where(lane == 1, length & 7, 0))
    leaving[tokens:] = tail.astype(jnp.float32).astype(jnp.bfloat16)
    fetches[0].wait()
    for fetch in fetches[2:]:
        fetch.wait()


def prepare(mig, lengths, pool, cache):
    rows, tokens, width = cache.shape
    smem = pl.BlockSpec(memory_space=pltpu.SMEM)
    vmem = pl.BlockSpec(memory_space=pltpu.VMEM)
    hbm = pl.BlockSpec(memory_space=pltpu.HBM)
    paired = jax.ShapeDtypeStruct((pool.shape[0] // 2, 2 * HD), pool.dtype)
    return pl.pallas_call(
        prepare_kernel,
        out_shape=[paired, paired, jax.ShapeDtypeStruct((tokens + TAIL, width), cache.dtype)],
        in_specs=[smem, hbm, hbm, hbm],
        out_specs=[vmem, vmem, vmem],
        scratch_shapes=[
            pltpu.SMEM(lengths.shape, lengths.dtype),
            pltpu.SemaphoreType.DMA((4 + pool.shape[0] // BLK,)),
        ],
        compiler_params=pltpu.CompilerParams(vmem_limit_bytes=8 * MIB),
        cost_estimate=pl.CostEstimate(
            flops=0, bytes_accessed=2 * (pool.size + tokens * width), transcendentals=0
        ),
        name="prepare",
    )(mig, in_hbm(lengths), in_hbm(pool), in_hbm(cache))


def resident_kernel(
    mig,
    lengths,
    queries_hbm,
    new_kv_hbm,
    prefix_hbm,
    moved,
    cache_hbm,
    out,
    belongs,
    cache,
    tail,
    new_kv,
    queries,
    prefix,
    flat,
    sems,
    small_sems,
):
    rows, tokens, _ = cache.shape
    small = [
        (queries_hbm, queries),
        (new_kv_hbm, new_kv),
        (prefix_hbm, prefix),
        (moved.at[pl.ds(tokens, TAIL)], tail),
    ]
    small = [pltpu.make_async_copy(*ends, small_sems.at[n]) for n, ends in enumerate(small)]
    for fetch in small:
        fetch.start()
    fetches = []
    for s in range(rows):
        here = pltpu.make_async_copy(cache_hbm.at[s], cache.at[s], sems.at[s])
        came = pltpu.make_async_copy(moved.at[pl.ds(0, tokens)], cache.at[s], sems.at[s])
        pl.when(mig[0] != s)(here.start)
        pl.when(mig[0] == s)(came.start)
        fetches.append(here)
    for fetch in small:
        fetch.wait()
    codes = slot_codes(prefix[...], belongs.shape[1] // CAP).astype(jnp.int32)
    belongs[...] = jnp.broadcast_to(jnp.where(codes < NONE, codes >> 7, -1), belongs.shape)
    parts = tail[...].astype(jnp.float32)
    moved_length = (parts[0:1, 0:1] * 8.0 + parts[0:1, 1:2]).astype(jnp.int32)
    length = [jnp.where(mig[0] == s, moved_length, lengths[s]) for s in range(rows)]
    own = queries[...].astype(jnp.float32)
    for g in range(GRP):
        flat[pl.ds(g, rows, stride=GRP), :] = own[:, g * HD : (g + 1) * HD]
    query = [flat[s * GRP : (s + 1) * GRP, :] for s in range(rows)]
    key = new_kv[:, :HD].astype(jnp.float32)
    fresh = [
        jnp.sum(query[s] * key[s : s + 1], axis=1, keepdims=True) * SCALE for s in range(rows)
    ]
    query = [q.astype(jnp.bfloat16) for q in query]
    for c in range(0, rows, TOGETHER):
        slots = range(c, c + TOGETHER)
        for s in slots:
            fetches[s].wait()
        mixes, stats = attend([query[s] for s in slots], cache, slots, [length[s] for s in slots])
        for s, mix, stat in zip(slots, mixes, stats):
            out[s, :GRP] = mix
            out[s, GRP:] = jnp.where(lanes((GRP, HD)) == 2, fresh[s], stat)


def resident(insts, mig, lengths, queries, new_kv, prefix, moved, cache):
    rows, tokens, width = cache.shape
    smem = pl.BlockSpec(memory_space=pltpu.SMEM)
    vmem = pl.BlockSpec(memory_space=pltpu.VMEM)
    hbm = pl.BlockSpec(memory_space=pltpu.HBM)
    return pl.pallas_call(
        resident_kernel,
        out_shape=[
            jax.ShapeDtypeStruct((rows, 2 * GRP, HD), jnp.float32),
            jax.ShapeDtypeStruct((GRP, CAP * insts), jnp.int32),
        ],
        in_specs=[smem, smem, hbm, hbm, hbm, pl.BlockSpec(memory_space=pl.ANY), hbm],
        out_specs=[vmem, vmem],
        scratch_shapes=[
            pltpu.VMEM(cache.shape, cache.dtype),
            pltpu.VMEM((TAIL, width), cache.dtype),
            pltpu.VMEM(new_kv.shape, new_kv.dtype),
            pltpu.VMEM(queries.shape, queries.dtype),
            pltpu.VMEM(prefix.shape, prefix.dtype),
            pltpu.VMEM((rows * GRP, HD), jnp.float32),
            pltpu.SemaphoreType.DMA((rows,)),
            pltpu.SemaphoreType.DMA((4,)),
        ],
        compiler_params=pltpu.CompilerParams(vmem_limit_bytes=12 * MIB),
        cost_estimate=pl.CostEstimate(
            flops=1 << 34, bytes_accessed=1 << 26, transcendentals=rows * GRP * tokens
        ),
        name="resident",
    )(mig, lengths, in_hbm(queries), in_hbm(new_kv), in_hbm(prefix), moved, in_hbm(cache))


def owner_kernel(arrived, keys, values, out, stage, packed, sems):
    stage[...] = arrived[...].astype(jnp.float32)
    insts = stage.shape[0] // ROWS
    slots = CAP * insts
    half = keys.shape[0] // BLK

    def rows_of(r):
        return stage[pl.ds(r, insts, stride=ROWS), :]

    ids = rows_of(CAP * GRP)
    local = jnp.concatenate([ids[:, k : k + 1] for k in range(CAP)], axis=0).astype(jnp.int32)
    local = jnp.broadcast_to(local, (slots, BLK))
    odd = (local & 1) == 1
    pair = jnp.concatenate([local >> 1] * HEADS, axis=0)
    rest = jnp.concatenate([local & (half - 1)] * HEADS, axis=0)
    upper = jnp.concatenate([local >= half] * HEADS, axis=0)
    lane = lanes((slots, HD))

    def score(c):
        query = []
        for g in range(c * HEADS, (c + 1) * HEADS):
            part = jnp.concatenate([rows_of(k * GRP + g) for k in range(CAP)], axis=0)
            halves = [jnp.where(odd, 0.0, part), jnp.where(odd, part, 0.0)]
            query.append(jnp.concatenate(halves, axis=1).astype(jnp.bfloat16))
        return dot(jnp.concatenate(query, axis=0), keys[...], NT)

    def weigh(scores):
        picked = scores[:, :BLK]
        for p in range(1, half):
            picked = jnp.where(pair == p, scores[:, p * BLK : (p + 1) * BLK], picked)
        picked = picked * SCALE
        peak = jnp.max(picked, axis=1, keepdims=True).astype(jnp.bfloat16).astype(jnp.float32)
        weights = jnp.exp(picked - peak)
        total = jnp.sum(weights, axis=1, keepdims=True)
        spread = [jnp.where(rest == b, weights, 0.0).astype(jnp.bfloat16) for b in range(half)]
        return jnp.concatenate(spread, axis=1), peak, total

    def mix(spread):
        both = dot(spread, values[...], NN)
        return jnp.where(upper, both[:, HD:], both[:, :HD])

    chunks = GRP // HEADS
    stats = jnp.zeros((slots, HD), jnp.float32)
    mixes = []
    scores = score(0)
    waiting = None
    for c in range(chunks):
        following = score(c + 1) if c + 1 < chunks else None
        spread, peak, total = weigh(scores)
        if waiting is not None:
            mixes.append(mix(waiting))
        total_hi = total.astype(jnp.bfloat16).astype(jnp.float32)
        total_lo = total - total_hi
        for h in range(HEADS):
            g = c * HEADS + h
            part = slice(h * slots, (h + 1) * slots)
            stats = jnp.where(lane == g, peak[part], stats)
            stats = jnp.where(lane == GRP + g, total_hi[part], stats)
            stats = jnp.where(lane == 2 * GRP + g, total_lo[part], stats)
        scores, waiting = following, spread
    mixes.append(mix(waiting))
    put = []
    for k in range(CAP):
        for g in range(GRP):
            start = g % HEADS * slots + k * insts
            put.append((k * GRP + g, mixes[g // HEADS][start : start + insts]))
        put.append((CAP * GRP + k, stats[k * insts : (k + 1) * insts]))
    send_out(put, insts, stage, packed, out, sems)


def owner(arrived, keys, values):
    vmem = pl.BlockSpec(memory_space=pltpu.VMEM)
    return pl.pallas_call(
        owner_kernel,
        out_shape=jax.ShapeDtypeStruct(arrived.shape, jnp.bfloat16),
        in_specs=[vmem, vmem, vmem],
        out_specs=pl.BlockSpec(memory_space=pl.ANY),
        scratch_shapes=[
            pltpu.VMEM(arrived.shape, jnp.float32),
            pltpu.VMEM(arrived.shape, jnp.bfloat16),
            pltpu.SemaphoreType.DMA((2,)),
        ],
        compiler_params=pltpu.CompilerParams(vmem_limit_bytes=24 * MIB),
        cost_estimate=pl.CostEstimate(
            flops=1 << 29, bytes_accessed=2 << 20, transcendentals=1 << 17
        ),
        name="owner",
    )(arrived, keys, values)


def combine_kernel(belongs, arrived, own, new_kv, out, wide, table):
    wide[...] = arrived[...].astype(jnp.float32)
    insts = wide.shape[0] // ROWS
    rows = own.shape[0]
    slots = CAP * insts

    def rows_of(r):
        return wide[pl.ds(r, insts, stride=ROWS), :]

    stats = jnp.concatenate([rows_of(CAP * GRP + k) for k in range(CAP)], axis=0).T
    peak = stats[:GRP]
    total = stats[GRP : 2 * GRP] + stats[2 * GRP : 3 * GRP]
    values = new_kv[:, HD:].astype(jnp.float32)
    below, mixes = [], []
    for s in range(rows):
        mine = belongs[...] == s
        stat = own[s, GRP:]
        res_peak, res_total, new_peak = stat[:, 0:1], stat[:, 1:2], stat[:, 2:3]
        top = jnp.max(jnp.where(mine, peak, LOW), axis=1, keepdims=True)
        top = jnp.maximum(jnp.maximum(top, res_peak), new_peak)
        weight = jnp.where(mine, jnp.exp(jnp.where(mine, peak, LOW) - top), 0.0)
        table[s * GRP : (s + 1) * GRP, :] = weight
        res_scale = jnp.exp(res_peak - top)
        new_scale = jnp.exp(new_peak - top)
        below.append(
            jnp.sum(weight * total, axis=1, keepdims=True) + res_scale * res_total + new_scale
        )
        mixes.append(
            res_scale * own[s, :GRP] + new_scale * values[s : s + 1]
        )
    sums = []
    for g in range(GRP):
        weight = table[pl.ds(g, rows, stride=GRP), :]
        weight_hi = weight.astype(jnp.bfloat16).astype(jnp.float32)
        both = jnp.concatenate([weight_hi, weight - weight_hi], axis=0).astype(jnp.bfloat16)
        mix = jnp.concatenate([rows_of(k * GRP + g) for k in range(CAP)], axis=0)
        got = dot(both, mix.astype(jnp.bfloat16), NN)
        sums.append(got[:rows] + got[rows:])
    for g in range(GRP):
        table[pl.ds(g, rows, stride=GRP), :] = sums[g]
    attended = [
        (table[s * GRP : (s + 1) * GRP, :] + mixes[s]) / below[s]
        for s in (r ^ FIRST_TP for r in range(rows))
    ]
    out[...] = jnp.concatenate(attended, axis=0).astype(jnp.bfloat16)


def combine(belongs, arrived, own, new_kv):
    rows = own.shape[0]
    vmem = pl.BlockSpec(memory_space=pltpu.VMEM)
    return pl.pallas_call(
        combine_kernel,
        out_shape=jax.ShapeDtypeStruct((rows * GRP, HD), jnp.bfloat16),
        in_specs=[vmem] * 4,
        out_specs=vmem,
        scratch_shapes=[
            pltpu.VMEM(arrived.shape, jnp.float32),
            pltpu.VMEM((rows * GRP, HD), jnp.float32),
        ],
        compiler_params=pltpu.CompilerParams(vmem_limit_bytes=8 * MIB),
        cost_estimate=pl.CostEstimate(flops=1 << 24, bytes_accessed=1 << 20, transcendentals=8192),
        name="combine",
    )(belongs, arrived, own, new_kv)


def on_device(queries, new_kv, cache, lengths, migrate_slot, pool, prefix_blocks):
    rows = queries.shape[0]
    insts = lax.axis_size("inst")
    swap = [(i, i ^ (insts // 2)) for i in range(insts)]
    order = [[r ^ FIRST for r in range(insts)]]
    order_tp = [[r ^ FIRST_TP for r in range(rows)]]

    def exchange(messages):
        messages = messages.reshape(insts, ROWS // 2, 2, HD)
        arrived = lax.all_to_all(
            messages, "inst", split_axis=0, concat_axis=0, axis_index_groups=order, tiled=True
        )
        return arrived.reshape(-1, HD)

    asked = exchange(pack(insts, prefix_blocks, queries))
    keys, values, leaving = prepare(migrate_slot, lengths, pool.reshape(-1, 2 * HD), cache)
    moved = lax.ppermute(leaving, "inst", swap)
    answers = exchange(owner(asked, keys, values))
    own, belongs = resident(
        insts, migrate_slot, lengths, queries, new_kv, prefix_blocks, moved, cache
    )
    attended = combine(belongs, answers, own, new_kv)
    attended = attended.reshape(rows, GRP, HD)
    heads = lax.all_to_all(
        attended, "tp", split_axis=0, concat_axis=0, axis_index_groups=order_tp, tiled=True
    )
    heads = jnp.concatenate([heads[FIRST_TP:], heads[:FIRST_TP]], axis=0)
    return heads.reshape(1, -1)


def solution(mesh):
    in_specs = (
        P("inst", "tp"),
        P("inst", "tp"),
        P("inst", None, "tp"),
        P("inst"),
        P("inst"),
        P("inst", None, "tp"),
        P("inst", None),
    )
    out_specs = P(("inst", "tp"), None)
    return jax.shard_map(
        on_device, mesh=mesh, in_specs=in_specs, out_specs=out_specs, check_vma=False
    )
```

```python
import jax
import jax.numpy as jnp
from jax import lax
from jax.experimental import pallas as pl
from jax.experimental.pallas import tpu as pltpu
from jax.sharding import PartitionSpec as P

QH = 64
KVH = 8
HD = 128
BLK = 128
GRP = QH // KVH
CAP = 2
NONE = 8191
FIRST = 20
FIRST_TP = 4
TAIL = 16
HEADS = 4
TOGETHER = 4
SPARE = 24
ROWS = 18
SCALE = HD**-0.5
LOW = -1e30
MIB = 1024 * 1024

NT = (((1,), (1,)), ((), ()))
NN = (((1,), (0,)), ((), ()))


def dot(a, b, dims):
    return lax.dot_general(a, b, dims, preferred_element_type=jnp.float32)


def in_hbm(x):
    return pltpu.with_memory_space_constraint(x, pltpu.HBM)


def lanes(shape):
    return lax.broadcasted_iota(jnp.int32, shape, len(shape) - 1)


def slot_codes(ids, insts):
    rows, width = ids.shape
    slots = CAP * insts
    lane = (lanes((rows, slots)) & (insts - 1)) ^ FIRST
    row = lax.broadcasted_iota(jnp.int32, (rows, slots), 0)
    first = jnp.full((rows, slots), NONE, jnp.int32)
    last = jnp.full((rows, slots), -1, jnp.int32)
    for e in range(width):
        entry = jnp.broadcast_to(ids[:, e : e + 1], (rows, slots))
        named = (entry >= 0) & ((entry >> 3) == lane)
        code = (row * width + e) * 8 + (entry & 7)
        first = jnp.where(named, jnp.minimum(first, code), first)
        last = jnp.where(named, code, last)
    first = jnp.min(first.astype(jnp.float32), axis=0, keepdims=True)
    last = jnp.max(last.astype(jnp.float32), axis=0, keepdims=True)
    second = jnp.where(last > first, last, float(NONE))
    return jnp.where(lanes((1, slots)) < insts, first, second)


def send_out(put, insts, stage, packed, out, sems):
    half = insts // 2
    copies = []
    for h in range(2):
        for r, part in put:
            first = h * half * ROWS + r
            stage[pl.ds(first, half, stride=ROWS), :] = part[h * half : (h + 1) * half]
        span = pl.ds(h * half * ROWS, half * ROWS)
        packed[span, :] = stage[span, :].astype(jnp.bfloat16)
        copies.append(pltpu.make_async_copy(packed.at[span], out.at[span], sems.at[h]))
        copies[h].start()
    for copy in copies:
        copy.wait()


def pack_kernel(prefix_hbm, queries_hbm, out, stage, packed, prefix, queries, sems, out_sems):
    fetch_prefix = pltpu.make_async_copy(prefix_hbm, prefix, sems.at[0])
    fetch_queries = pltpu.make_async_copy(queries_hbm, queries, sems.at[1])
    fetch_prefix.start()
    fetch_queries.start()
    insts = packed.shape[0] // ROWS
    slots = CAP * insts
    fetch_prefix.wait()
    codes = jnp.broadcast_to(slot_codes(prefix[...], insts), (slots, slots)).T.astype(jnp.int32)
    pick = ((codes >> 7) == lanes(codes.shape))[:, :GRP].astype(jnp.float32).astype(jnp.bfloat16)
    fetch_queries.wait()
    picked = dot(pick, queries[...], NN)
    lane = lanes((insts, HD))
    local = (codes & 7).astype(jnp.float32)
    ids = jnp.where(lane == 0, local[:insts], jnp.where(lane == 1, local[insts:], 0.0))
    put = [
        (k * GRP + g, picked[k * insts : (k + 1) * insts, g * HD : (g + 1) * HD])
        for k in range(CAP)
        for g in range(GRP)
    ]
    put.append((CAP * GRP, ids))
    put.append((CAP * GRP + 1, jnp.zeros((insts, HD), jnp.float32)))
    send_out(put, insts, stage, packed, out, out_sems)


def pack(insts, prefix, queries):
    size = insts * ROWS
    hbm = pl.BlockSpec(memory_space=pltpu.HBM)
    return pl.pallas_call(
        pack_kernel,
        out_shape=jax.ShapeDtypeStruct((size, HD), jnp.bfloat16),
        in_specs=[hbm, hbm],
        out_specs=pl.BlockSpec(memory_space=pl.ANY),
        scratch_shapes=[
            pltpu.VMEM((size + SPARE, HD), jnp.float32),
            pltpu.VMEM((size, HD), jnp.bfloat16),
            pltpu.VMEM(prefix.shape, prefix.dtype),
            pltpu.VMEM(queries.shape, queries.dtype),
            pltpu.SemaphoreType.DMA((2,)),
            pltpu.SemaphoreType.DMA((2,)),
        ],
        compiler_params=pltpu.CompilerParams(vmem_limit_bytes=8 * MIB),
        cost_estimate=pl.CostEstimate(flops=1 << 22, bytes_accessed=1 << 19, transcendentals=0),
        name="pack",
    )(in_hbm(prefix), in_hbm(queries))


def attend(queries, cache, slots, lengths):
    scores = [dot(q, cache[s, :, :HD], NT) * SCALE for q, s in zip(queries, slots)]
    valid = [lanes(x.shape) < jnp.broadcast_to(n, x.shape) for x, n in zip(scores, lengths)]
    peaks = [
        jnp.max(jnp.where(v, x, LOW), axis=1, keepdims=True) for x, v in zip(scores, valid)
    ]
    weights = [jnp.where(v, jnp.exp(x - p), 0.0) for x, v, p in zip(scores, valid, peaks)]
    mixes = [dot(w.astype(jnp.bfloat16), cache[s, :, HD:], NN) for w, s in zip(weights, slots)]
    totals = [jnp.sum(w, axis=1, keepdims=True) for w in weights]
    stats = [jnp.where(lanes((GRP, HD)) == 0, p, t) for p, t in zip(peaks, totals)]
    return mixes, stats


def prepare_kernel(mig, lengths_hbm, pool, cache, keys, values, leaving, lengths, sems):
    tokens = cache.shape[1]
    fetches = [
        (cache.at[mig[0]], leaving.at[pl.ds(0, tokens)]),
        (lengths_hbm, lengths),
    ]
    half = keys.shape[0] // BLK
    for b in range(2):
        lanes_of = pl.ds(b * HD, HD)
        part = pl.ds(b * half * BLK, half * BLK)
        fetches.append((pool.at[part, pl.ds(HD, HD)], values.at[:, lanes_of]))
        for p in range(half):
            block = pl.ds((2 * p + b) * BLK, BLK)
            fetches.append((pool.at[block, pl.ds(0, HD)], keys.at[pl.ds(p * BLK, BLK), lanes_of]))
    fetches = [pltpu.make_async_copy(*ends, sems.at[n]) for n, ends in enumerate(fetches)]
    for fetch in fetches:
        fetch.start()
    fetches[1].wait()
    length = lengths[mig[0]]
    lane = lanes((TAIL, leaving.shape[1]))
    tail = jnp.where(lane == 0, length >> 3, jnp.where(lane == 1, length & 7, 0))
    leaving[tokens:] = tail.astype(jnp.float32).astype(jnp.bfloat16)
    fetches[0].wait()
    for fetch in fetches[2:]:
        fetch.wait()


def prepare(mig, lengths, pool, cache):
    rows, tokens, width = cache.shape
    smem = pl.BlockSpec(memory_space=pltpu.SMEM)
    vmem = pl.BlockSpec(memory_space=pltpu.VMEM)
    hbm = pl.BlockSpec(memory_space=pltpu.HBM)
    paired = jax.ShapeDtypeStruct((pool.shape[0] // 2, 2 * HD), pool.dtype)
    return pl.pallas_call(
        prepare_kernel,
        out_shape=[paired, paired, jax.ShapeDtypeStruct((tokens + TAIL, width), cache.dtype)],
        in_specs=[smem, hbm, hbm, hbm],
        out_specs=[vmem, vmem, vmem],
        scratch_shapes=[
            pltpu.SMEM(lengths.shape, lengths.dtype),
            pltpu.SemaphoreType.DMA((4 + pool.shape[0] // BLK,)),
        ],
        compiler_params=pltpu.CompilerParams(vmem_limit_bytes=8 * MIB),
        cost_estimate=pl.CostEstimate(
            flops=0, bytes_accessed=2 * (pool.size + tokens * width), transcendentals=0
        ),
        name="prepare",
    )(mig, in_hbm(lengths), in_hbm(pool), in_hbm(cache))


def resident_kernel(
    mig,
    lengths,
    queries_hbm,
    new_kv_hbm,
    prefix_hbm,
    moved,
    cache_hbm,
    out,
    belongs,
    cache,
    tail,
    new_kv,
    queries,
    prefix,
    flat,
    sems,
    small_sems,
):
    rows, tokens, _ = cache.shape
    small = [
        (queries_hbm, queries),
        (new_kv_hbm, new_kv),
        (prefix_hbm, prefix),
        (moved.at[pl.ds(tokens, TAIL)], tail),
    ]
    small = [pltpu.make_async_copy(*ends, small_sems.at[n]) for n, ends in enumerate(small)]
    for fetch in small:
        fetch.start()
    fetches = []
    for s in range(rows):
        here = pltpu.make_async_copy(cache_hbm.at[s], cache.at[s], sems.at[s])
        came = pltpu.make_async_copy(moved.at[pl.ds(0, tokens)], cache.at[s], sems.at[s])
        pl.when(mig[0] != s)(here.start)
        pl.when(mig[0] == s)(came.start)
        fetches.append(here)
    for fetch in small:
        fetch.wait()
    codes = slot_codes(prefix[...], belongs.shape[1] // CAP).astype(jnp.int32)
    belongs[...] = jnp.broadcast_to(jnp.where(codes < NONE, codes >> 7, -1), belongs.shape)
    parts = tail[...].astype(jnp.float32)
    moved_length = (parts[0:1, 0:1] * 8.0 + parts[0:1, 1:2]).astype(jnp.int32)
    length = [jnp.where(mig[0] == s, moved_length, lengths[s]) for s in range(rows)]
    own = queries[...].astype(jnp.float32)
    for g in range(GRP):
        flat[pl.ds(g, rows, stride=GRP), :] = own[:, g * HD : (g + 1) * HD]
    query = [flat[s * GRP : (s + 1) * GRP, :] for s in range(rows)]
    key = new_kv[:, :HD].astype(jnp.float32)
    fresh = [
        jnp.sum(query[s] * key[s : s + 1], axis=1, keepdims=True) * SCALE for s in range(rows)
    ]
    query = [q.astype(jnp.bfloat16) for q in query]
    for c in range(0, rows, TOGETHER):
        slots = range(c, c + TOGETHER)
        for s in slots:
            fetches[s].wait()
        mixes, stats = attend([query[s] for s in slots], cache, slots, [length[s] for s in slots])
        for s, mix, stat in zip(slots, mixes, stats):
            out[s, :GRP] = mix
            out[s, GRP:] = jnp.where(lanes((GRP, HD)) == 2, fresh[s], stat)


def resident(insts, mig, lengths, queries, new_kv, prefix, moved, cache):
    rows, tokens, width = cache.shape
    smem = pl.BlockSpec(memory_space=pltpu.SMEM)
    vmem = pl.BlockSpec(memory_space=pltpu.VMEM)
    hbm = pl.BlockSpec(memory_space=pltpu.HBM)
    return pl.pallas_call(
        resident_kernel,
        out_shape=[
            jax.ShapeDtypeStruct((rows, 2 * GRP, HD), jnp.float32),
            jax.ShapeDtypeStruct((GRP, CAP * insts), jnp.int32),
        ],
        in_specs=[smem, smem, hbm, hbm, hbm, pl.BlockSpec(memory_space=pl.ANY), hbm],
        out_specs=[vmem, vmem],
        scratch_shapes=[
            pltpu.VMEM(cache.shape, cache.dtype),
            pltpu.VMEM((TAIL, width), cache.dtype),
            pltpu.VMEM(new_kv.shape, new_kv.dtype),
            pltpu.VMEM(queries.shape, queries.dtype),
            pltpu.VMEM(prefix.shape, prefix.dtype),
            pltpu.VMEM((rows * GRP + SPARE, HD), jnp.float32),
            pltpu.SemaphoreType.DMA((rows,)),
            pltpu.SemaphoreType.DMA((4,)),
        ],
        compiler_params=pltpu.CompilerParams(vmem_limit_bytes=12 * MIB),
        cost_estimate=pl.CostEstimate(
            flops=1 << 34, bytes_accessed=1 << 26, transcendentals=rows * GRP * tokens
        ),
        name="resident",
    )(mig, lengths, in_hbm(queries), in_hbm(new_kv), in_hbm(prefix), moved, in_hbm(cache))


def owner_kernel(arrived, keys, values, out, stage, packed, sems):
    size = arrived.shape[0]
    stage[:size] = arrived[...].astype(jnp.float32)
    insts = size // ROWS
    slots = CAP * insts
    half = keys.shape[0] // BLK

    def rows_of(r):
        return stage[pl.ds(r, insts, stride=ROWS), :]

    ids = rows_of(CAP * GRP)
    local = jnp.concatenate([ids[:, k : k + 1] for k in range(CAP)], axis=0).astype(jnp.int32)
    local = jnp.broadcast_to(local, (slots, BLK))
    odd = (local & 1) == 1
    pair = jnp.concatenate([local >> 1] * HEADS, axis=0)
    rest = jnp.concatenate([local & (half - 1)] * HEADS, axis=0)
    upper = jnp.concatenate([local >= half] * HEADS, axis=0)
    lane = lanes((slots, HD))

    def score(c):
        query = []
        for g in range(c * HEADS, (c + 1) * HEADS):
            part = jnp.concatenate([rows_of(k * GRP + g) for k in range(CAP)], axis=0)
            halves = [jnp.where(odd, 0.0, part), jnp.where(odd, part, 0.0)]
            query.append(jnp.concatenate(halves, axis=1).astype(jnp.bfloat16))
        return dot(jnp.concatenate(query, axis=0), keys[...], NT)

    def weigh(scores):
        picked = scores[:, :BLK]
        for p in range(1, half):
            picked = jnp.where(pair == p, scores[:, p * BLK : (p + 1) * BLK], picked)
        picked = picked * SCALE
        peak = jnp.max(picked, axis=1, keepdims=True).astype(jnp.bfloat16).astype(jnp.float32)
        weights = jnp.exp(picked - peak)
        total = jnp.sum(weights, axis=1, keepdims=True)
        spread = [jnp.where(rest == b, weights, 0.0).astype(jnp.bfloat16) for b in range(half)]
        return jnp.concatenate(spread, axis=1), peak, total

    def mix(spread):
        both = dot(spread, values[...], NN)
        return jnp.where(upper, both[:, HD:], both[:, :HD])

    chunks = GRP // HEADS
    stats = jnp.zeros((slots, HD), jnp.float32)
    mixes = []
    scores = score(0)
    waiting = None
    for c in range(chunks):
        following = score(c + 1) if c + 1 < chunks else None
        spread, peak, total = weigh(scores)
        if waiting is not None:
            mixes.append(mix(waiting))
        total_hi = total.astype(jnp.bfloat16).astype(jnp.float32)
        total_lo = total - total_hi
        for h in range(HEADS):
            g = c * HEADS + h
            part = slice(h * slots, (h + 1) * slots)
            stats = jnp.where(lane == g, peak[part], stats)
            stats = jnp.where(lane == GRP + g, total_hi[part], stats)
            stats = jnp.where(lane == 2 * GRP + g, total_lo[part], stats)
        scores, waiting = following, spread
    mixes.append(mix(waiting))
    put = []
    for k in range(CAP):
        for g in range(GRP):
            start = g % HEADS * slots + k * insts
            put.append((k * GRP + g, mixes[g // HEADS][start : start + insts]))
        put.append((CAP * GRP + k, stats[k * insts : (k + 1) * insts]))
    send_out(put, insts, stage, packed, out, sems)


def owner(arrived, keys, values):
    vmem = pl.BlockSpec(memory_space=pltpu.VMEM)
    return pl.pallas_call(
        owner_kernel,
        out_shape=jax.ShapeDtypeStruct(arrived.shape, jnp.bfloat16),
        in_specs=[vmem, vmem, vmem],
        out_specs=pl.BlockSpec(memory_space=pl.ANY),
        scratch_shapes=[
            pltpu.VMEM((arrived.shape[0] + SPARE, HD), jnp.float32),
            pltpu.VMEM(arrived.shape, jnp.bfloat16),
            pltpu.SemaphoreType.DMA((2,)),
        ],
        compiler_params=pltpu.CompilerParams(vmem_limit_bytes=24 * MIB),
        cost_estimate=pl.CostEstimate(
            flops=1 << 29, bytes_accessed=2 << 20, transcendentals=1 << 17
        ),
        name="owner",
    )(arrived, keys, values)


def combine_kernel(belongs, arrived, own, new_kv, out, wide, table):
    size = arrived.shape[0]
    wide[:size] = arrived[...].astype(jnp.float32)
    insts = size // ROWS
    rows = own.shape[0]
    slots = CAP * insts

    def rows_of(r):
        return wide[pl.ds(r, insts, stride=ROWS), :]

    stats = jnp.concatenate([rows_of(CAP * GRP + k) for k in range(CAP)], axis=0).T
    peak = stats[:GRP]
    total = stats[GRP : 2 * GRP] + stats[2 * GRP : 3 * GRP]
    values = new_kv[:, HD:].astype(jnp.float32)
    below, mixes = [], []
    for s in range(rows):
        mine = belongs[...] == s
        stat = own[s, GRP:]
        res_peak, res_total, new_peak = stat[:, 0:1], stat[:, 1:2], stat[:, 2:3]
        top = jnp.max(jnp.where(mine, peak, LOW), axis=1, keepdims=True)
        top = jnp.maximum(jnp.maximum(top, res_peak), new_peak)
        weight = jnp.where(mine, jnp.exp(jnp.where(mine, peak, LOW) - top), 0.0)
        table[s * GRP : (s + 1) * GRP, :] = weight
        res_scale = jnp.exp(res_peak - top)
        new_scale = jnp.exp(new_peak - top)
        below.append(
            jnp.sum(weight * total, axis=1, keepdims=True) + res_scale * res_total + new_scale
        )
        mixes.append(
            res_scale * own[s, :GRP] + new_scale * values[s : s + 1]
        )
    sums = []
    for g in range(GRP):
        weight = table[pl.ds(g, rows, stride=GRP), :]
        weight_hi = weight.astype(jnp.bfloat16).astype(jnp.float32)
        both = jnp.concatenate([weight_hi, weight - weight_hi], axis=0).astype(jnp.bfloat16)
        mix = jnp.concatenate([rows_of(k * GRP + g) for k in range(CAP)], axis=0)
        got = dot(both, mix.astype(jnp.bfloat16), NN)
        sums.append(got[:rows] + got[rows:])
    for g in range(GRP):
        table[pl.ds(g, rows, stride=GRP), :] = sums[g]
    attended = [
        (table[s * GRP : (s + 1) * GRP, :] + mixes[s]) / below[s]
        for s in (r ^ FIRST_TP for r in range(rows))
    ]
    out[...] = jnp.concatenate(attended, axis=0).astype(jnp.bfloat16)


def combine(belongs, arrived, own, new_kv):
    rows = own.shape[0]
    vmem = pl.BlockSpec(memory_space=pltpu.VMEM)
    return pl.pallas_call(
        combine_kernel,
        out_shape=jax.ShapeDtypeStruct((rows * GRP, HD), jnp.bfloat16),
        in_specs=[vmem] * 4,
        out_specs=vmem,
        scratch_shapes=[
            pltpu.VMEM((arrived.shape[0] + SPARE, HD), jnp.float32),
            pltpu.VMEM((rows * GRP + SPARE, HD), jnp.float32),
        ],
        compiler_params=pltpu.CompilerParams(vmem_limit_bytes=8 * MIB),
        cost_estimate=pl.CostEstimate(flops=1 << 24, bytes_accessed=1 << 20, transcendentals=8192),
        name="combine",
    )(belongs, arrived, own, new_kv)


def on_device(queries, new_kv, cache, lengths, migrate_slot, pool, prefix_blocks):
    rows = queries.shape[0]
    insts = lax.axis_size("inst")
    swap = [(i, i ^ (insts // 2)) for i in range(insts)]
    order = [[r ^ FIRST for r in range(insts)]]
    order_tp = [[r ^ FIRST_TP for r in range(rows)]]

    def exchange(messages):
        messages = messages.reshape(insts, ROWS // 2, 2, HD)
        arrived = lax.all_to_all(
            messages, "inst", split_axis=0, concat_axis=0, axis_index_groups=order, tiled=True
        )
        return arrived.reshape(-1, HD)

    asked = exchange(pack(insts, prefix_blocks, queries))
    keys, values, leaving = prepare(migrate_slot, lengths, pool.reshape(-1, 2 * HD), cache)
    moved = lax.ppermute(leaving, "inst", swap)
    answers = exchange(owner(asked, keys, values))
    own, belongs = resident(
        insts, migrate_slot, lengths, queries, new_kv, prefix_blocks, moved, cache
    )
    attended = combine(belongs, answers, own, new_kv)
    attended = attended.reshape(rows, GRP, HD)
    heads = lax.all_to_all(
        attended, "tp", split_axis=0, concat_axis=0, axis_index_groups=order_tp, tiled=True
    )
    heads = jnp.concatenate([heads[FIRST_TP:], heads[:FIRST_TP]], axis=0)
    return heads.reshape(1, -1)


def solution(mesh):
    in_specs = (
        P("inst", "tp"),
        P("inst", "tp"),
        P("inst", None, "tp"),
        P("inst"),
        P("inst"),
        P("inst", None, "tp"),
        P("inst", None),
    )
    out_specs = P(("inst", "tp"), None)
    return jax.shard_map(
        on_device, mesh=mesh, in_specs=in_specs, out_specs=out_specs, check_vma=False
    )
```

```python
import jax
import jax.numpy as jnp
from jax import lax
from jax.experimental import pallas as pl
from jax.experimental.pallas import tpu as pltpu
from jax.sharding import PartitionSpec as P

QH = 64
KVH = 8
HD = 128
BLK = 128
GRP = QH // KVH
CAP = 2
NONE = 8191
LEAD_X, LEAD_Z = 2, 4
FIRST_TP = 4
TAIL = 16
HEADS = 4
TOGETHER = 4
SPARE = 24
ROWS = 18
SCALE = HD**-0.5
LOW = -1e30
MIB = 1024 * 1024

NT = (((1,), (1,)), ((), ()))
NN = (((1,), (0,)), ((), ()))


def dot(a, b, dims):
    return lax.dot_general(a, b, dims, preferred_element_type=jnp.float32)


def in_hbm(x):
    return pltpu.with_memory_space_constraint(x, pltpu.HBM)


def lanes(shape):
    return lax.broadcasted_iota(jnp.int32, shape, len(shape) - 1)


def step(n):
    half = (n + 1) >> 1
    return half * (2 * (n & 1) - 1)


def member(r):
    z = (LEAD_Z + step(r >> 3)) & 7
    x = (LEAD_X + step((r >> 1) & 3)) & 3
    return ((r & 1) * 4 + x) * 8 + z


def slot_codes(ids, insts):
    rows, width = ids.shape
    slots = CAP * insts
    lane = member(lanes((rows, slots)) & (insts - 1))
    row = lax.broadcasted_iota(jnp.int32, (rows, slots), 0)
    first = jnp.full((rows, slots), NONE, jnp.int32)
    last = jnp.full((rows, slots), -1, jnp.int32)
    for e in range(width):
        entry = jnp.broadcast_to(ids[:, e : e + 1], (rows, slots))
        named = (entry >= 0) & ((entry >> 3) == lane)
        code = (row * width + e) * 8 + (entry & 7)
        first = jnp.where(named, jnp.minimum(first, code), first)
        last = jnp.where(named, code, last)
    first = jnp.min(first.astype(jnp.float32), axis=0, keepdims=True)
    last = jnp.max(last.astype(jnp.float32), axis=0, keepdims=True)
    second = jnp.where(last > first, last, float(NONE))
    return jnp.where(lanes((1, slots)) < insts, first, second)


def send_out(put, insts, stage, packed, out, sems):
    half = insts // 2
    copies = []
    for h in range(2):
        for r, part in put:
            first = h * half * ROWS + r
            stage[pl.ds(first, half, stride=ROWS), :] = part[h * half : (h + 1) * half]
        span = pl.ds(h * half * ROWS, half * ROWS)
        packed[span, :] = stage[span, :].astype(jnp.bfloat16)
        copies.append(pltpu.make_async_copy(packed.at[span], out.at[span], sems.at[h]))
        copies[h].start()
    for copy in copies:
        copy.wait()


def pack_kernel(prefix_hbm, queries_hbm, out, stage, packed, prefix, queries, sems, out_sems):
    fetch_prefix = pltpu.make_async_copy(prefix_hbm, prefix, sems.at[0])
    fetch_queries = pltpu.make_async_copy(queries_hbm, queries, sems.at[1])
    fetch_prefix.start()
    fetch_queries.start()
    insts = packed.shape[0] // ROWS
    slots = CAP * insts
    fetch_prefix.wait()
    codes = jnp.broadcast_to(slot_codes(prefix[...], insts), (slots, slots)).T.astype(jnp.int32)
    pick = ((codes >> 7) == lanes(codes.shape))[:, :GRP].astype(jnp.float32).astype(jnp.bfloat16)
    fetch_queries.wait()
    picked = dot(pick, queries[...], NN)
    lane = lanes((insts, HD))
    local = (codes & 7).astype(jnp.float32)
    ids = jnp.where(lane == 0, local[:insts], jnp.where(lane == 1, local[insts:], 0.0))
    put = [
        (k * GRP + g, picked[k * insts : (k + 1) * insts, g * HD : (g + 1) * HD])
        for k in range(CAP)
        for g in range(GRP)
    ]
    put.append((CAP * GRP, ids))
    put.append((CAP * GRP + 1, jnp.zeros((insts, HD), jnp.float32)))
    send_out(put, insts, stage, packed, out, out_sems)


def pack(insts, prefix, queries):
    size = insts * ROWS
    hbm = pl.BlockSpec(memory_space=pltpu.HBM)
    return pl.pallas_call(
        pack_kernel,
        out_shape=jax.ShapeDtypeStruct((size, HD), jnp.bfloat16),
        in_specs=[hbm, hbm],
        out_specs=pl.BlockSpec(memory_space=pl.ANY),
        scratch_shapes=[
            pltpu.VMEM((size + SPARE, HD), jnp.float32),
            pltpu.VMEM((size, HD), jnp.bfloat16),
            pltpu.VMEM(prefix.shape, prefix.dtype),
            pltpu.VMEM(queries.shape, queries.dtype),
            pltpu.SemaphoreType.DMA((2,)),
            pltpu.SemaphoreType.DMA((2,)),
        ],
        compiler_params=pltpu.CompilerParams(vmem_limit_bytes=8 * MIB),
        cost_estimate=pl.CostEstimate(flops=1 << 22, bytes_accessed=1 << 19, transcendentals=0),
        name="pack",
    )(in_hbm(prefix), in_hbm(queries))


def attend(queries, cache, slots, lengths):
    scores = [dot(q, cache[s, :, :HD], NT) * SCALE for q, s in zip(queries, slots)]
    valid = [lanes(x.shape) < jnp.broadcast_to(n, x.shape) for x, n in zip(scores, lengths)]
    peaks = [
        jnp.max(jnp.where(v, x, LOW), axis=1, keepdims=True) for x, v in zip(scores, valid)
    ]
    weights = [jnp.where(v, jnp.exp(x - p), 0.0) for x, v, p in zip(scores, valid, peaks)]
    mixes = [dot(w.astype(jnp.bfloat16), cache[s, :, HD:], NN) for w, s in zip(weights, slots)]
    totals = [jnp.sum(w, axis=1, keepdims=True) for w in weights]
    stats = [jnp.where(lanes((GRP, HD)) == 0, p, t) for p, t in zip(peaks, totals)]
    return mixes, stats


def prepare_kernel(mig, lengths_hbm, pool, cache, keys, values, leaving, lengths, sems):
    tokens = cache.shape[1]
    fetches = [
        (cache.at[mig[0]], leaving.at[pl.ds(0, tokens)]),
        (lengths_hbm, lengths),
    ]
    half = keys.shape[0] // BLK
    for b in range(2):
        lanes_of = pl.ds(b * HD, HD)
        part = pl.ds(b * half * BLK, half * BLK)
        fetches.append((pool.at[part, pl.ds(HD, HD)], values.at[:, lanes_of]))
        for p in range(half):
            block = pl.ds((2 * p + b) * BLK, BLK)
            fetches.append((pool.at[block, pl.ds(0, HD)], keys.at[pl.ds(p * BLK, BLK), lanes_of]))
    fetches = [pltpu.make_async_copy(*ends, sems.at[n]) for n, ends in enumerate(fetches)]
    for fetch in fetches:
        fetch.start()
    fetches[1].wait()
    length = lengths[mig[0]]
    lane = lanes((TAIL, leaving.shape[1]))
    tail = jnp.where(lane == 0, length >> 3, jnp.where(lane == 1, length & 7, 0))
    leaving[tokens:] = tail.astype(jnp.float32).astype(jnp.bfloat16)
    fetches[0].wait()
    for fetch in fetches[2:]:
        fetch.wait()


def prepare(mig, lengths, pool, cache):
    rows, tokens, width = cache.shape
    smem = pl.BlockSpec(memory_space=pltpu.SMEM)
    vmem = pl.BlockSpec(memory_space=pltpu.VMEM)
    hbm = pl.BlockSpec(memory_space=pltpu.HBM)
    paired = jax.ShapeDtypeStruct((pool.shape[0] // 2, 2 * HD), pool.dtype)
    return pl.pallas_call(
        prepare_kernel,
        out_shape=[paired, paired, jax.ShapeDtypeStruct((tokens + TAIL, width), cache.dtype)],
        in_specs=[smem, hbm, hbm, hbm],
        out_specs=[vmem, vmem, vmem],
        scratch_shapes=[
            pltpu.SMEM(lengths.shape, lengths.dtype),
            pltpu.SemaphoreType.DMA((4 + pool.shape[0] // BLK,)),
        ],
        compiler_params=pltpu.CompilerParams(vmem_limit_bytes=8 * MIB),
        cost_estimate=pl.CostEstimate(
            flops=0, bytes_accessed=2 * (pool.size + tokens * width), transcendentals=0
        ),
        name="prepare",
    )(mig, in_hbm(lengths), in_hbm(pool), in_hbm(cache))


def resident_kernel(
    mig,
    lengths,
    queries_hbm,
    new_kv_hbm,
    prefix_hbm,
    moved,
    cache_hbm,
    out,
    belongs,
    cache,
    tail,
    new_kv,
    queries,
    prefix,
    flat,
    sems,
    small_sems,
):
    rows, tokens, _ = cache.shape
    small = [
        (queries_hbm, queries),
        (new_kv_hbm, new_kv),
        (prefix_hbm, prefix),
        (moved.at[pl.ds(tokens, TAIL)], tail),
    ]
    small = [pltpu.make_async_copy(*ends, small_sems.at[n]) for n, ends in enumerate(small)]
    for fetch in small:
        fetch.start()
    fetches = []
    for s in range(rows):
        here = pltpu.make_async_copy(cache_hbm.at[s], cache.at[s], sems.at[s])
        came = pltpu.make_async_copy(moved.at[pl.ds(0, tokens)], cache.at[s], sems.at[s])
        pl.when(mig[0] != s)(here.start)
        pl.when(mig[0] == s)(came.start)
        fetches.append(here)
    for fetch in small:
        fetch.wait()
    codes = slot_codes(prefix[...], belongs.shape[1] // CAP).astype(jnp.int32)
    belongs[...] = jnp.broadcast_to(jnp.where(codes < NONE, codes >> 7, -1), belongs.shape)
    parts = tail[...].astype(jnp.float32)
    moved_length = (parts[0:1, 0:1] * 8.0 + parts[0:1, 1:2]).astype(jnp.int32)
    length = [jnp.where(mig[0] == s, moved_length, lengths[s]) for s in range(rows)]
    own = queries[...].astype(jnp.float32)
    for g in range(GRP):
        flat[pl.ds(g, rows, stride=GRP), :] = own[:, g * HD : (g + 1) * HD]
    query = [flat[s * GRP : (s + 1) * GRP, :] for s in range(rows)]
    key = new_kv[:, :HD].astype(jnp.float32)
    fresh = [
        jnp.sum(query[s] * key[s : s + 1], axis=1, keepdims=True) * SCALE for s in range(rows)
    ]
    query = [q.astype(jnp.bfloat16) for q in query]
    for c in range(0, rows, TOGETHER):
        slots = range(c, c + TOGETHER)
        for s in slots:
            fetches[s].wait()
        mixes, stats = attend([query[s] for s in slots], cache, slots, [length[s] for s in slots])
        for s, mix, stat in zip(slots, mixes, stats):
            out[s, :GRP] = mix
            out[s, GRP:] = jnp.where(lanes((GRP, HD)) == 2, fresh[s], stat)


def resident(insts, mig, lengths, queries, new_kv, prefix, moved, cache):
    rows, tokens, width = cache.shape
    smem = pl.BlockSpec(memory_space=pltpu.SMEM)
    vmem = pl.BlockSpec(memory_space=pltpu.VMEM)
    hbm = pl.BlockSpec(memory_space=pltpu.HBM)
    return pl.pallas_call(
        resident_kernel,
        out_shape=[
            jax.ShapeDtypeStruct((rows, 2 * GRP, HD), jnp.float32),
            jax.ShapeDtypeStruct((GRP, CAP * insts), jnp.int32),
        ],
        in_specs=[smem, smem, hbm, hbm, hbm, pl.BlockSpec(memory_space=pl.ANY), hbm],
        out_specs=[vmem, vmem],
        scratch_shapes=[
            pltpu.VMEM(cache.shape, cache.dtype),
            pltpu.VMEM((TAIL, width), cache.dtype),
            pltpu.VMEM(new_kv.shape, new_kv.dtype),
            pltpu.VMEM(queries.shape, queries.dtype),
            pltpu.VMEM(prefix.shape, prefix.dtype),
            pltpu.VMEM((rows * GRP + SPARE, HD), jnp.float32),
            pltpu.SemaphoreType.DMA((rows,)),
            pltpu.SemaphoreType.DMA((4,)),
        ],
        compiler_params=pltpu.CompilerParams(vmem_limit_bytes=12 * MIB),
        cost_estimate=pl.CostEstimate(
            flops=1 << 34, bytes_accessed=1 << 26, transcendentals=rows * GRP * tokens
        ),
        name="resident",
    )(mig, lengths, in_hbm(queries), in_hbm(new_kv), in_hbm(prefix), moved, in_hbm(cache))


def owner_kernel(arrived, keys, values, out, stage, packed, sems):
    size = arrived.shape[0]
    stage[:size] = arrived[...].astype(jnp.float32)
    insts = size // ROWS
    slots = CAP * insts
    half = keys.shape[0] // BLK

    def rows_of(r):
        return stage[pl.ds(r, insts, stride=ROWS), :]

    ids = rows_of(CAP * GRP)
    local = jnp.concatenate([ids[:, k : k + 1] for k in range(CAP)], axis=0).astype(jnp.int32)
    local = jnp.broadcast_to(local, (slots, BLK))
    odd = (local & 1) == 1
    pair = jnp.concatenate([local >> 1] * HEADS, axis=0)
    rest = jnp.concatenate([local & (half - 1)] * HEADS, axis=0)
    upper = jnp.concatenate([local >= half] * HEADS, axis=0)
    lane = lanes((slots, HD))

    def score(c):
        query = []
        for g in range(c * HEADS, (c + 1) * HEADS):
            part = jnp.concatenate([rows_of(k * GRP + g) for k in range(CAP)], axis=0)
            halves = [jnp.where(odd, 0.0, part), jnp.where(odd, part, 0.0)]
            query.append(jnp.concatenate(halves, axis=1).astype(jnp.bfloat16))
        return dot(jnp.concatenate(query, axis=0), keys[...], NT)

    def weigh(scores):
        picked = scores[:, :BLK]
        for p in range(1, half):
            picked = jnp.where(pair == p, scores[:, p * BLK : (p + 1) * BLK], picked)
        picked = picked * SCALE
        peak = jnp.max(picked, axis=1, keepdims=True).astype(jnp.bfloat16).astype(jnp.float32)
        weights = jnp.exp(picked - peak)
        total = jnp.sum(weights, axis=1, keepdims=True)
        spread = [jnp.where(rest == b, weights, 0.0).astype(jnp.bfloat16) for b in range(half)]
        return jnp.concatenate(spread, axis=1), peak, total

    def mix(spread):
        both = dot(spread, values[...], NN)
        return jnp.where(upper, both[:, HD:], both[:, :HD])

    chunks = GRP // HEADS
    stats = jnp.zeros((slots, HD), jnp.float32)
    mixes = []
    scores = score(0)
    waiting = None
    for c in range(chunks):
        following = score(c + 1) if c + 1 < chunks else None
        spread, peak, total = weigh(scores)
        if waiting is not None:
            mixes.append(mix(waiting))
        total_hi = total.astype(jnp.bfloat16).astype(jnp.float32)
        total_lo = total - total_hi
        for h in range(HEADS):
            g = c * HEADS + h
            part = slice(h * slots, (h + 1) * slots)
            stats = jnp.where(lane == g, peak[part], stats)
            stats = jnp.where(lane == GRP + g, total_hi[part], stats)
            stats = jnp.where(lane == 2 * GRP + g, total_lo[part], stats)
        scores, waiting = following, spread
    mixes.append(mix(waiting))
    put = []
    for k in range(CAP):
        for g in range(GRP):
            start = g % HEADS * slots + k * insts
            put.append((k * GRP + g, mixes[g // HEADS][start : start + insts]))
        put.append((CAP * GRP + k, stats[k * insts : (k + 1) * insts]))
    send_out(put, insts, stage, packed, out, sems)


def owner(arrived, keys, values):
    vmem = pl.BlockSpec(memory_space=pltpu.VMEM)
    return pl.pallas_call(
        owner_kernel,
        out_shape=jax.ShapeDtypeStruct(arrived.shape, jnp.bfloat16),
        in_specs=[vmem, vmem, vmem],
        out_specs=pl.BlockSpec(memory_space=pl.ANY),
        scratch_shapes=[
            pltpu.VMEM((arrived.shape[0] + SPARE, HD), jnp.float32),
            pltpu.VMEM(arrived.shape, jnp.bfloat16),
            pltpu.SemaphoreType.DMA((2,)),
        ],
        compiler_params=pltpu.CompilerParams(vmem_limit_bytes=24 * MIB),
        cost_estimate=pl.CostEstimate(
            flops=1 << 29, bytes_accessed=2 << 20, transcendentals=1 << 17
        ),
        name="owner",
    )(arrived, keys, values)


def combine_kernel(belongs, arrived, own, new_kv, out, wide, table):
    size = arrived.shape[0]
    wide[:size] = arrived[...].astype(jnp.float32)
    insts = size // ROWS
    rows = own.shape[0]
    slots = CAP * insts

    def rows_of(r):
        return wide[pl.ds(r, insts, stride=ROWS), :]

    stats = jnp.concatenate([rows_of(CAP * GRP + k) for k in range(CAP)], axis=0).T
    peak = stats[:GRP]
    total = stats[GRP : 2 * GRP] + stats[2 * GRP : 3 * GRP]
    values = new_kv[:, HD:].astype(jnp.float32)
    below, mixes = [], []
    for s in range(rows):
        mine = belongs[...] == s
        stat = own[s, GRP:]
        res_peak, res_total, new_peak = stat[:, 0:1], stat[:, 1:2], stat[:, 2:3]
        top = jnp.max(jnp.where(mine, peak, LOW), axis=1, keepdims=True)
        top = jnp.maximum(jnp.maximum(top, res_peak), new_peak)
        weight = jnp.where(mine, jnp.exp(jnp.where(mine, peak, LOW) - top), 0.0)
        table[s * GRP : (s + 1) * GRP, :] = weight
        res_scale = jnp.exp(res_peak - top)
        new_scale = jnp.exp(new_peak - top)
        below.append(
            jnp.sum(weight * total, axis=1, keepdims=True) + res_scale * res_total + new_scale
        )
        mixes.append(
            res_scale * own[s, :GRP] + new_scale * values[s : s + 1]
        )
    sums = []
    for g in range(GRP):
        weight = table[pl.ds(g, rows, stride=GRP), :]
        weight_hi = weight.astype(jnp.bfloat16).astype(jnp.float32)
        both = jnp.concatenate([weight_hi, weight - weight_hi], axis=0).astype(jnp.bfloat16)
        mix = jnp.concatenate([rows_of(k * GRP + g) for k in range(CAP)], axis=0)
        got = dot(both, mix.astype(jnp.bfloat16), NN)
        sums.append(got[:rows] + got[rows:])
    for g in range(GRP):
        table[pl.ds(g, rows, stride=GRP), :] = sums[g]
    attended = [
        (table[s * GRP : (s + 1) * GRP, :] + mixes[s]) / below[s]
        for s in (r ^ FIRST_TP for r in range(rows))
    ]
    out[...] = jnp.concatenate(attended, axis=0).astype(jnp.bfloat16)


def combine(belongs, arrived, own, new_kv):
    rows = own.shape[0]
    vmem = pl.BlockSpec(memory_space=pltpu.VMEM)
    return pl.pallas_call(
        combine_kernel,
        out_shape=jax.ShapeDtypeStruct((rows * GRP, HD), jnp.bfloat16),
        in_specs=[vmem] * 4,
        out_specs=vmem,
        scratch_shapes=[
            pltpu.VMEM((arrived.shape[0] + SPARE, HD), jnp.float32),
            pltpu.VMEM((rows * GRP + SPARE, HD), jnp.float32),
        ],
        compiler_params=pltpu.CompilerParams(vmem_limit_bytes=8 * MIB),
        cost_estimate=pl.CostEstimate(flops=1 << 24, bytes_accessed=1 << 20, transcendentals=8192),
        name="combine",
    )(belongs, arrived, own, new_kv)


def on_device(queries, new_kv, cache, lengths, migrate_slot, pool, prefix_blocks):
    rows = queries.shape[0]
    insts = lax.axis_size("inst")
    swap = [(i, i ^ (insts // 2)) for i in range(insts)]
    order = [[member(r) for r in range(insts)]]
    order_tp = [[r ^ FIRST_TP for r in range(rows)]]

    def exchange(messages):
        messages = messages.reshape(insts, ROWS // 2, 2, HD)
        arrived = lax.all_to_all(
            messages, "inst", split_axis=0, concat_axis=0, axis_index_groups=order, tiled=True
        )
        return arrived.reshape(-1, HD)

    asked = exchange(pack(insts, prefix_blocks, queries))
    keys, values, leaving = prepare(migrate_slot, lengths, pool.reshape(-1, 2 * HD), cache)
    moved = lax.ppermute(leaving, "inst", swap)
    answers = exchange(owner(asked, keys, values))
    own, belongs = resident(
        insts, migrate_slot, lengths, queries, new_kv, prefix_blocks, moved, cache
    )
    attended = combine(belongs, answers, own, new_kv)
    attended = attended.reshape(rows, GRP, HD)
    heads = lax.all_to_all(
        attended, "tp", split_axis=0, concat_axis=0, axis_index_groups=order_tp, tiled=True
    )
    heads = jnp.concatenate([heads[FIRST_TP:], heads[:FIRST_TP]], axis=0)
    return heads.reshape(1, -1)


def solution(mesh):
    in_specs = (
        P("inst", "tp"),
        P("inst", "tp"),
        P("inst", None, "tp"),
        P("inst"),
        P("inst"),
        P("inst", None, "tp"),
        P("inst", None),
    )
    out_specs = P(("inst", "tp"), None)
    return jax.shard_map(
        on_device, mesh=mesh, in_specs=in_specs, out_specs=out_specs, check_vma=False
    )
```

```python
import jax
import jax.numpy as jnp
from jax import lax
from jax.experimental import pallas as pl
from jax.experimental.pallas import tpu as pltpu
from jax.sharding import PartitionSpec as P

QH = 64
KVH = 8
HD = 128
BLK = 128
GRP = QH // KVH
CAP = 2
NONE = 8191
FIRST = 21
FIRST_TP = 4
TAIL = 16
HEADS = 4
TOGETHER = 4
SPARE = 24
ROWS = 18
SCALE = HD**-0.5
LOW = -1e30
MIB = 1024 * 1024

NT = (((1,), (1,)), ((), ()))
NN = (((1,), (0,)), ((), ()))


def dot(a, b, dims):
    return lax.dot_general(a, b, dims, preferred_element_type=jnp.float32)


def in_hbm(x):
    return pltpu.with_memory_space_constraint(x, pltpu.HBM)


def lanes(shape):
    return lax.broadcasted_iota(jnp.int32, shape, len(shape) - 1)


def slot_codes(ids, insts):
    rows, width = ids.shape
    slots = CAP * insts
    lane = (lanes((rows, slots)) & (insts - 1)) ^ FIRST
    row = lax.broadcasted_iota(jnp.int32, (rows, slots), 0)
    first = jnp.full((rows, slots), NONE, jnp.int32)
    last = jnp.full((rows, slots), -1, jnp.int32)
    for e in range(width):
        entry = jnp.broadcast_to(ids[:, e : e + 1], (rows, slots))
        named = (entry >= 0) & ((entry >> 3) == lane)
        code = (row * width + e) * 8 + (entry & 7)
        first = jnp.where(named, jnp.minimum(first, code), first)
        last = jnp.where(named, code, last)
    first = jnp.min(first.astype(jnp.float32), axis=0, keepdims=True)
    last = jnp.max(last.astype(jnp.float32), axis=0, keepdims=True)
    second = jnp.where(last > first, last, float(NONE))
    return jnp.where(lanes((1, slots)) < insts, first, second)


def send_out(put, insts, stage, packed, out, sems):
    half = insts // 2
    copies = []
    for h in range(2):
        for r, part in put:
            first = h * half * ROWS + r
            stage[pl.ds(first, half, stride=ROWS), :] = part[h * half : (h + 1) * half]
        span = pl.ds(h * half * ROWS, half * ROWS)
        packed[span, :] = stage[span, :].astype(jnp.bfloat16)
        copies.append(pltpu.make_async_copy(packed.at[span], out.at[span], sems.at[h]))
        copies[h].start()
    for copy in copies:
        copy.wait()


def pack_kernel(prefix_hbm, queries_hbm, out, stage, packed, prefix, queries, sems, out_sems):
    fetch_prefix = pltpu.make_async_copy(prefix_hbm, prefix, sems.at[0])
    fetch_queries = pltpu.make_async_copy(queries_hbm, queries, sems.at[1])
    fetch_prefix.start()
    fetch_queries.start()
    insts = packed.shape[0] // ROWS
    slots = CAP * insts
    fetch_prefix.wait()
    codes = jnp.broadcast_to(slot_codes(prefix[...], insts), (slots, slots)).T.astype(jnp.int32)
    pick = ((codes >> 7) == lanes(codes.shape))[:, :GRP].astype(jnp.float32).astype(jnp.bfloat16)
    fetch_queries.wait()
    picked = dot(pick, queries[...], NN)
    lane = lanes((insts, HD))
    local = (codes & 7).astype(jnp.float32)
    ids = jnp.where(lane == 0, local[:insts], jnp.where(lane == 1, local[insts:], 0.0))
    put = [
        (k * GRP + g, picked[k * insts : (k + 1) * insts, g * HD : (g + 1) * HD])
        for k in range(CAP)
        for g in range(GRP)
    ]
    put.append((CAP * GRP, ids))
    put.append((CAP * GRP + 1, jnp.zeros((insts, HD), jnp.float32)))
    send_out(put, insts, stage, packed, out, out_sems)


def pack(insts, prefix, queries):
    size = insts * ROWS
    hbm = pl.BlockSpec(memory_space=pltpu.HBM)
    return pl.pallas_call(
        pack_kernel,
        out_shape=jax.ShapeDtypeStruct((size, HD), jnp.bfloat16),
        in_specs=[hbm, hbm],
        out_specs=pl.BlockSpec(memory_space=pl.ANY),
        scratch_shapes=[
            pltpu.VMEM((size + SPARE, HD), jnp.float32),
            pltpu.VMEM((size, HD), jnp.bfloat16),
            pltpu.VMEM(prefix.shape, prefix.dtype),
            pltpu.VMEM(queries.shape, queries.dtype),
            pltpu.SemaphoreType.DMA((2,)),
            pltpu.SemaphoreType.DMA((2,)),
        ],
        compiler_params=pltpu.CompilerParams(vmem_limit_bytes=8 * MIB),
        cost_estimate=pl.CostEstimate(flops=1 << 22, bytes_accessed=1 << 19, transcendentals=0),
        name="pack",
    )(in_hbm(prefix), in_hbm(queries))


def attend(queries, cache, slots, lengths):
    scores = [dot(q, cache[s, :, :HD], NT) * SCALE for q, s in zip(queries, slots)]
    valid = [lanes(x.shape) < jnp.broadcast_to(n, x.shape) for x, n in zip(scores, lengths)]
    peaks = [
        jnp.max(jnp.where(v, x, LOW), axis=1, keepdims=True) for x, v in zip(scores, valid)
    ]
    weights = [jnp.where(v, jnp.exp(x - p), 0.0) for x, v, p in zip(scores, valid, peaks)]
    mixes = [dot(w.astype(jnp.bfloat16), cache[s, :, HD:], NN) for w, s in zip(weights, slots)]
    totals = [jnp.sum(w, axis=1, keepdims=True) for w in weights]
    stats = [jnp.where(lanes((GRP, HD)) == 0, p, t) for p, t in zip(peaks, totals)]
    return mixes, stats


def prepare_kernel(mig, lengths_hbm, pool, cache, keys, values, leaving, lengths, sems):
    tokens = cache.shape[1]
    fetches = [
        (cache.at[mig[0]], leaving.at[pl.ds(0, tokens)]),
        (lengths_hbm, lengths),
    ]
    half = keys.shape[0] // BLK
    for b in range(2):
        lanes_of = pl.ds(b * HD, HD)
        part = pl.ds(b * half * BLK, half * BLK)
        fetches.append((pool.at[part, pl.ds(HD, HD)], values.at[:, lanes_of]))
        for p in range(half):
            block = pl.ds((2 * p + b) * BLK, BLK)
            fetches.append((pool.at[block, pl.ds(0, HD)], keys.at[pl.ds(p * BLK, BLK), lanes_of]))
    fetches = [pltpu.make_async_copy(*ends, sems.at[n]) for n, ends in enumerate(fetches)]
    for fetch in fetches:
        fetch.start()
    fetches[1].wait()
    length = lengths[mig[0]]
    lane = lanes((TAIL, leaving.shape[1]))
    tail = jnp.where(lane == 0, length >> 3, jnp.where(lane == 1, length & 7, 0))
    leaving[tokens:] = tail.astype(jnp.float32).astype(jnp.bfloat16)
    fetches[0].wait()
    for fetch in fetches[2:]:
        fetch.wait()


def prepare(mig, lengths, pool, cache):
    rows, tokens, width = cache.shape
    smem = pl.BlockSpec(memory_space=pltpu.SMEM)
    vmem = pl.BlockSpec(memory_space=pltpu.VMEM)
    hbm = pl.BlockSpec(memory_space=pltpu.HBM)
    paired = jax.ShapeDtypeStruct((pool.shape[0] // 2, 2 * HD), pool.dtype)
    return pl.pallas_call(
        prepare_kernel,
        out_shape=[paired, paired, jax.ShapeDtypeStruct((tokens + TAIL, width), cache.dtype)],
        in_specs=[smem, hbm, hbm, hbm],
        out_specs=[vmem, vmem, vmem],
        scratch_shapes=[
            pltpu.SMEM(lengths.shape, lengths.dtype),
            pltpu.SemaphoreType.DMA((4 + pool.shape[0] // BLK,)),
        ],
        compiler_params=pltpu.CompilerParams(vmem_limit_bytes=8 * MIB),
        cost_estimate=pl.CostEstimate(
            flops=0, bytes_accessed=2 * (pool.size + tokens * width), transcendentals=0
        ),
        name="prepare",
    )(mig, in_hbm(lengths), in_hbm(pool), in_hbm(cache))


def resident_kernel(
    mig,
    lengths,
    queries_hbm,
    new_kv_hbm,
    prefix_hbm,
    moved,
    cache_hbm,
    out,
    belongs,
    cache,
    tail,
    new_kv,
    queries,
    prefix,
    flat,
    sems,
    small_sems,
):
    rows, tokens, _ = cache.shape
    small = [
        (queries_hbm, queries),
        (new_kv_hbm, new_kv),
        (prefix_hbm, prefix),
        (moved.at[pl.ds(tokens, TAIL)], tail),
    ]
    small = [pltpu.make_async_copy(*ends, small_sems.at[n]) for n, ends in enumerate(small)]
    for fetch in small:
        fetch.start()
    fetches = []
    for s in range(rows):
        here = pltpu.make_async_copy(cache_hbm.at[s], cache.at[s], sems.at[s])
        came = pltpu.make_async_copy(moved.at[pl.ds(0, tokens)], cache.at[s], sems.at[s])
        pl.when(mig[0] != s)(here.start)
        pl.when(mig[0] == s)(came.start)
        fetches.append(here)
    for fetch in small:
        fetch.wait()
    codes = slot_codes(prefix[...], belongs.shape[1] // CAP).astype(jnp.int32)
    belongs[...] = jnp.broadcast_to(jnp.where(codes < NONE, codes >> 7, -1), belongs.shape)
    parts = tail[...].astype(jnp.float32)
    moved_length = (parts[0:1, 0:1] * 8.0 + parts[0:1, 1:2]).astype(jnp.int32)
    length = [jnp.where(mig[0] == s, moved_length, lengths[s]) for s in range(rows)]
    own = queries[...].astype(jnp.float32)
    for g in range(GRP):
        flat[pl.ds(g, rows, stride=GRP), :] = own[:, g * HD : (g + 1) * HD]
    query = [flat[s * GRP : (s + 1) * GRP, :] for s in range(rows)]
    key = new_kv[:, :HD].astype(jnp.float32)
    fresh = [
        jnp.sum(query[s] * key[s : s + 1], axis=1, keepdims=True) * SCALE for s in range(rows)
    ]
    query = [q.astype(jnp.bfloat16) for q in query]
    for c in range(0, rows, TOGETHER):
        slots = range(c, c + TOGETHER)
        for s in slots:
            fetches[s].wait()
        mixes, stats = attend([query[s] for s in slots], cache, slots, [length[s] for s in slots])
        for s, mix, stat in zip(slots, mixes, stats):
            out[s, :GRP] = mix
            out[s, GRP:] = jnp.where(lanes((GRP, HD)) == 2, fresh[s], stat)


def resident(insts, mig, lengths, queries, new_kv, prefix, moved, cache):
    rows, tokens, width = cache.shape
    smem = pl.BlockSpec(memory_space=pltpu.SMEM)
    vmem = pl.BlockSpec(memory_space=pltpu.VMEM)
    hbm = pl.BlockSpec(memory_space=pltpu.HBM)
    return pl.pallas_call(
        resident_kernel,
        out_shape=[
            jax.ShapeDtypeStruct((rows, 2 * GRP, HD), jnp.float32),
            jax.ShapeDtypeStruct((GRP, CAP * insts), jnp.int32),
        ],
        in_specs=[smem, smem, hbm, hbm, hbm, pl.BlockSpec(memory_space=pl.ANY), hbm],
        out_specs=[vmem, vmem],
        scratch_shapes=[
            pltpu.VMEM(cache.shape, cache.dtype),
            pltpu.VMEM((TAIL, width), cache.dtype),
            pltpu.VMEM(new_kv.shape, new_kv.dtype),
            pltpu.VMEM(queries.shape, queries.dtype),
            pltpu.VMEM(prefix.shape, prefix.dtype),
            pltpu.VMEM((rows * GRP + SPARE, HD), jnp.float32),
            pltpu.SemaphoreType.DMA((rows,)),
            pltpu.SemaphoreType.DMA((4,)),
        ],
        compiler_params=pltpu.CompilerParams(vmem_limit_bytes=12 * MIB),
        cost_estimate=pl.CostEstimate(
            flops=1 << 34, bytes_accessed=1 << 26, transcendentals=rows * GRP * tokens
        ),
        name="resident",
    )(mig, lengths, in_hbm(queries), in_hbm(new_kv), in_hbm(prefix), moved, in_hbm(cache))


def owner_kernel(arrived, keys, values, out, stage, packed, sems):
    size = arrived.shape[0]
    stage[:size] = arrived[...].astype(jnp.float32)
    insts = size // ROWS
    slots = CAP * insts
    half = keys.shape[0] // BLK

    def rows_of(r):
        return stage[pl.ds(r, insts, stride=ROWS), :]

    ids = rows_of(CAP * GRP)
    local = jnp.concatenate([ids[:, k : k + 1] for k in range(CAP)], axis=0).astype(jnp.int32)
    local = jnp.broadcast_to(local, (slots, BLK))
    odd = (local & 1) == 1
    pair = jnp.concatenate([local >> 1] * HEADS, axis=0)
    rest = jnp.concatenate([local & (half - 1)] * HEADS, axis=0)
    upper = jnp.concatenate([local >= half] * HEADS, axis=0)
    lane = lanes((slots, HD))

    def score(c):
        query = []
        for g in range(c * HEADS, (c + 1) * HEADS):
            part = jnp.concatenate([rows_of(k * GRP + g) for k in range(CAP)], axis=0)
            halves = [jnp.where(odd, 0.0, part), jnp.where(odd, part, 0.0)]
            query.append(jnp.concatenate(halves, axis=1).astype(jnp.bfloat16))
        return dot(jnp.concatenate(query, axis=0), keys[...], NT)

    def weigh(scores):
        picked = scores[:, :BLK]
        for p in range(1, half):
            picked = jnp.where(pair == p, scores[:, p * BLK : (p + 1) * BLK], picked)
        picked = picked * SCALE
        peak = jnp.max(picked, axis=1, keepdims=True).astype(jnp.bfloat16).astype(jnp.float32)
        weights = jnp.exp(picked - peak)
        total = jnp.sum(weights, axis=1, keepdims=True)
        spread = [jnp.where(rest == b, weights, 0.0).astype(jnp.bfloat16) for b in range(half)]
        return jnp.concatenate(spread, axis=1), peak, total

    def mix(spread):
        both = dot(spread, values[...], NN)
        return jnp.where(upper, both[:, HD:], both[:, :HD])

    chunks = GRP // HEADS
    stats = jnp.zeros((slots, HD), jnp.float32)
    mixes = []
    scores = score(0)
    waiting = None
    for c in range(chunks):
        following = score(c + 1) if c + 1 < chunks else None
        spread, peak, total = weigh(scores)
        if waiting is not None:
            mixes.append(mix(waiting))
        total_hi = total.astype(jnp.bfloat16).astype(jnp.float32)
        total_lo = total - total_hi
        for h in range(HEADS):
            g = c * HEADS + h
            part = slice(h * slots, (h + 1) * slots)
            stats = jnp.where(lane == g, peak[part], stats)
            stats = jnp.where(lane == GRP + g, total_hi[part], stats)
            stats = jnp.where(lane == 2 * GRP + g, total_lo[part], stats)
        scores, waiting = following, spread
    mixes.append(mix(waiting))
    put = []
    for k in range(CAP):
        for g in range(GRP):
            start = g % HEADS * slots + k * insts
            put.append((k * GRP + g, mixes[g // HEADS][start : start + insts]))
        put.append((CAP * GRP + k, stats[k * insts : (k + 1) * insts]))
    send_out(put, insts, stage, packed, out, sems)


def owner(arrived, keys, values):
    vmem = pl.BlockSpec(memory_space=pltpu.VMEM)
    return pl.pallas_call(
        owner_kernel,
        out_shape=jax.ShapeDtypeStruct(arrived.shape, jnp.bfloat16),
        in_specs=[vmem, vmem, vmem],
        out_specs=pl.BlockSpec(memory_space=pl.ANY),
        scratch_shapes=[
            pltpu.VMEM((arrived.shape[0] + SPARE, HD), jnp.float32),
            pltpu.VMEM(arrived.shape, jnp.bfloat16),
            pltpu.SemaphoreType.DMA((2,)),
        ],
        compiler_params=pltpu.CompilerParams(vmem_limit_bytes=24 * MIB),
        cost_estimate=pl.CostEstimate(
            flops=1 << 29, bytes_accessed=2 << 20, transcendentals=1 << 17
        ),
        name="owner",
    )(arrived, keys, values)


def combine_kernel(belongs, arrived, own, new_kv, out, wide, table):
    size = arrived.shape[0]
    wide[:size] = arrived[...].astype(jnp.float32)
    insts = size // ROWS
    rows = own.shape[0]
    slots = CAP * insts

    def rows_of(r):
        return wide[pl.ds(r, insts, stride=ROWS), :]

    stats = jnp.concatenate([rows_of(CAP * GRP + k) for k in range(CAP)], axis=0).T
    peak = stats[:GRP]
    total = stats[GRP : 2 * GRP] + stats[2 * GRP : 3 * GRP]
    values = new_kv[:, HD:].astype(jnp.float32)
    below, mixes = [], []
    for s in range(rows):
        mine = belongs[...] == s
        stat = own[s, GRP:]
        res_peak, res_total, new_peak = stat[:, 0:1], stat[:, 1:2], stat[:, 2:3]
        top = jnp.max(jnp.where(mine, peak, LOW), axis=1, keepdims=True)
        top = jnp.maximum(jnp.maximum(top, res_peak), new_peak)
        weight = jnp.where(mine, jnp.exp(jnp.where(mine, peak, LOW) - top), 0.0)
        table[s * GRP : (s + 1) * GRP, :] = weight
        res_scale = jnp.exp(res_peak - top)
        new_scale = jnp.exp(new_peak - top)
        below.append(
            jnp.sum(weight * total, axis=1, keepdims=True) + res_scale * res_total + new_scale
        )
        mixes.append(
            res_scale * own[s, :GRP] + new_scale * values[s : s + 1]
        )
    sums = []
    for g in range(GRP):
        weight = table[pl.ds(g, rows, stride=GRP), :]
        weight_hi = weight.astype(jnp.bfloat16).astype(jnp.float32)
        both = jnp.concatenate([weight_hi, weight - weight_hi], axis=0).astype(jnp.bfloat16)
        mix = jnp.concatenate([rows_of(k * GRP + g) for k in range(CAP)], axis=0)
        got = dot(both, mix.astype(jnp.bfloat16), NN)
        sums.append(got[:rows] + got[rows:])
    for g in range(GRP):
        table[pl.ds(g, rows, stride=GRP), :] = sums[g]
    attended = [
        (table[s * GRP : (s + 1) * GRP, :] + mixes[s]) / below[s]
        for s in (r ^ FIRST_TP for r in range(rows))
    ]
    out[...] = jnp.concatenate(attended, axis=0).astype(jnp.bfloat16)


def combine(belongs, arrived, own, new_kv):
    rows = own.shape[0]
    vmem = pl.BlockSpec(memory_space=pltpu.VMEM)
    return pl.pallas_call(
        combine_kernel,
        out_shape=jax.ShapeDtypeStruct((rows * GRP, HD), jnp.bfloat16),
        in_specs=[vmem] * 4,
        out_specs=vmem,
        scratch_shapes=[
            pltpu.VMEM((arrived.shape[0] + SPARE, HD), jnp.float32),
            pltpu.VMEM((rows * GRP + SPARE, HD), jnp.float32),
        ],
        compiler_params=pltpu.CompilerParams(vmem_limit_bytes=8 * MIB),
        cost_estimate=pl.CostEstimate(flops=1 << 24, bytes_accessed=1 << 20, transcendentals=8192),
        name="combine",
    )(belongs, arrived, own, new_kv)


def on_device(queries, new_kv, cache, lengths, migrate_slot, pool, prefix_blocks):
    rows = queries.shape[0]
    insts = lax.axis_size("inst")
    swap = [(i, i ^ (insts // 2)) for i in range(insts)]
    order = [[r ^ FIRST for r in range(insts)]]
    order_tp = [[r ^ FIRST_TP for r in range(rows)]]

    def exchange(messages):
        messages = messages.reshape(insts, ROWS // 2, 2, HD)
        arrived = lax.all_to_all(
            messages, "inst", split_axis=0, concat_axis=0, axis_index_groups=order, tiled=True
        )
        return arrived.reshape(-1, HD)

    asked = exchange(pack(insts, prefix_blocks, queries))
    keys, values, leaving = prepare(migrate_slot, lengths, pool.reshape(-1, 2 * HD), cache)
    moved = lax.ppermute(leaving, "inst", swap)
    answers = exchange(owner(asked, keys, values))
    own, belongs = resident(
        insts, migrate_slot, lengths, queries, new_kv, prefix_blocks, moved, cache
    )
    attended = combine(belongs, answers, own, new_kv)
    attended = attended.reshape(rows, GRP, HD)
    heads = lax.all_to_all(
        attended, "tp", split_axis=0, concat_axis=0, axis_index_groups=order_tp, tiled=True
    )
    heads = jnp.concatenate([heads[FIRST_TP:], heads[:FIRST_TP]], axis=0)
    return heads.reshape(1, -1)


def solution(mesh):
    in_specs = (
        P("inst", "tp"),
        P("inst", "tp"),
        P("inst", None, "tp"),
        P("inst"),
        P("inst"),
        P("inst", None, "tp"),
        P("inst", None),
    )
    out_specs = P(("inst", "tp"), None)
    return jax.shard_map(
        on_device, mesh=mesh, in_specs=in_specs, out_specs=out_specs, check_vma=False
    )
```
